512 devices in a mesh: pts: 128 (over z, x, core), head: 4 (over y).
Axes of the slice: x: 4, y: 4, z: 16, core: 2. Of those that a mesh axis runs over, the one named last changes fastest.
Arguments:
- query_pool: bfloat16 [73728, 768], P('pts', 'head'), may hold values from -24 to 24
- sample_index: int32 [36864], P('pts'), may hold values from 0 to 575
- labels: int32 [36864], P('pts'), may hold values 0 or 1
- w_query: bfloat16 [768, 768], P(None, 'head'), may hold values from -0.21875 to 0.21875
- keys: bfloat16 [1024, 768], P('pts', 'head'), may hold values from -121.5 to 121.5
- values: bfloat16 [1024, 768], P('pts', 'head'), may hold values from -6 to 6
- w_out: bfloat16 [768, 768], P('head'), may hold values from -0.21875 to 0.21875
- out_gain: bfloat16 [768], replicated, may hold values from 0.099609375 to 1.8984375
- w_hidden: bfloat16 [768, 1536], P(None, 'head'), may hold values from -0.21875 to 0.21875
- w_logit: bfloat16 [1536], P('head'), may hold values from -0.15625 to 0.15625
Outputs:
- grad_query_weight: float32 [768, 768], P(None, 'head')
- grad_out_weight: float32 [768, 768], P('head')
- grad_hidden_weight: float32 [768, 1536], P(None, 'head')
- grad_logit_weight: float32 [1536], P('head')
- grad_gain: float32 [768], replicated
- grad_keys: float32 [1024, 768], P('pts', 'head')
- grad_values: float32 [1024, 768], P('pts', 'head')
The draws below stay inside these ranges and needn't reach their ends.
Inputs may be any that keep to these rules, and one draw needn't show every extreme that they name: `sample_index`: each entry names a row of the block of 576 candidate rows that holds its point's block, counted from that block's start.
All inputs are finite; a program needn't handle non-finite values. No bound on the sum of `labels` on one device may be relied on, other than what follows from the above.
Results may differ from the reference program's by a relative error of at most 0.03.
Values may be sent and summed in bfloat16 or wider, within the bound.
A program may use at most 64 MiB of HBM per device.

```python
import jax
import jax.numpy as jnp
from jax import lax

D = 768
HEADS = 12
HD = 64
FF = 1536
LAT = 1024
P_DEV = 288
POOL_DEV = 576
POINTS = 36864
POOL = 73728
N_PTS = 128


def draw_keys(key, part):
    key = jax.random.fold_in(key, 11)
    base = jnp.clip(jax.random.normal(key, (LAT, D), jnp.float32), -6.0, 6.0)
    return base.astype(jnp.bfloat16)


def plant(result, rng, least, high):
    dims = result.shape
    spot = [jax.random.randint(jax.random.fold_in(rng, axis), (), 0, dims[axis]) for axis in range(len(dims))]
    result = result.at[tuple(spot)].set(least)
    longest = dims.index(max(dims))
    spot[longest] = (spot[longest] + 1) % dims[longest]
    return result.at[tuple(spot)].set(high)


def strengthened(entries, key, source, target, blocks, factor):
    owner, partner = [(jnp.arange(entries.shape[axis_at]) // (entries.shape[axis_at] // blocks)).reshape([-1 if axis == axis_at else 1 for axis in range(entries.ndim)]) for axis_at in (source, target)]
    chosen = jax.random.permutation(key, blocks)[partner]
    strong = (owner == chosen) | (owner == (partner + blocks // 2) % blocks)
    return jnp.where(strong, factor * entries, entries)


def block_levels(key, shape, pieces, low, top_value):
    def one(dim, blocks):
        heights = jax.random.uniform(jax.random.fold_in(jax.random.fold_in(key, 6), dim), (blocks,), jnp.float32, low / len(pieces), top_value / len(pieces))
        return jnp.repeat(jnp.exp(heights), shape[dim] // blocks).reshape((-1,) + (1,) * (len(shape) - dim - 1))

    loudness = one(*pieces[0])
    for cut in pieces[1:]:
        loudness = loudness * one(*cut)
    return loudness


def bell_draw(key, extent, width, bound, split=(), held_as=jnp.bfloat16):
    loudness = block_levels(key, extent, split, -0.22, 0.18) if split else 1.0
    drawn = jax.random.normal(key, extent, jnp.float32) * width * loudness
    return jnp.minimum(jnp.maximum(drawn, -bound), bound).astype(held_as)


def gaussian_with(stream_key, extent, width, bound, shards, heavy, held_as=jnp.bfloat16):
    values = width * jax.random.normal(stream_key, extent, jnp.float32)
    if shards:
        values = values * block_levels(stream_key, extent, shards, -0.22, 0.18)
    return jnp.clip(strengthened(values, jax.random.fold_in(stream_key, 3), *heavy), -bound, bound).astype(held_as)


def setup_inputs(seed: int = 0) -> dict:
    key_list = jax.random.split(jax.random.key(seed), 11)
    query_pool = gaussian_with(key_list[0], (POOL, D), 1.0, 24.0, ((0, 128), (1, 4)), (0, 1, 128, 5.5))
    sample_index = plant(jax.random.randint(key_list[1], (POINTS,), 0, POOL_DEV), jax.random.fold_in(key_list[1], 1), 0, POOL_DEV - 1).astype(jnp.int32)
    labels = plant((jax.random.randint(key_list[2], (POINTS,), 0, 2) < 1).astype(jnp.int32), jax.random.fold_in(key_list[2], 1), 0, 1)
    w_query = bell_draw(key_list[3], (D, D), D ** -0.5, 0.21875, ((1, 4),))
    keys = draw_keys(jax.random.fold_in(key_list[10], 71), 0)
    values = bell_draw(key_list[5], (LAT, D), 1.0, 6.0, ((0, 128), (1, 4)))
    w_out = bell_draw(key_list[6], (D, D), D ** -0.5, 0.21875, ((0, 4),))
    out_gain = jnp.clip(1.0 + 0.18 * jax.random.normal(key_list[7], (D,), jnp.float32), 0.099609375, 1.8984375).astype(jnp.bfloat16)
    w_hidden = bell_draw(key_list[8], (D, FF), D ** -0.5, 0.21875, ((1, 4),))
    w_logit = bell_draw(key_list[9], (FF,), FF ** -0.5, 0.15625, ((0, 4),))
    return {"query_pool": query_pool, "sample_index": sample_index, "labels": labels, "w_query": w_query, "keys": keys, "values": values, "w_out": w_out, "out_gain": out_gain, "w_hidden": w_hidden, "w_logit": w_logit}


EPSILON = 1e-05

def reference(query_pool, sample_index, labels, w_query, keys, values, w_out, out_gain, w_hidden, w_logit):
    scale = HD ** (-0.5)
    pool_blocks = query_pool.reshape(N_PTS, POOL_DEV, D)
    index_blocks = sample_index.reshape(N_PTS, P_DEV)
    label_blocks = labels.reshape(N_PTS, P_DEV)
    key_heads = keys.astype(jnp.float32).reshape(LAT, HEADS, HD)
    value_heads = values.astype(jnp.float32).reshape(LAT, HEADS, HD)
    gain = out_gain.astype(jnp.float32)
    inv_root = POINTS ** (-0.5)

    def step(carry, block):
        pool_rows, index_rows, label_rows = block
        rows_in = jnp.take(pool_rows, index_rows.astype(jnp.int32), axis=0)
        query = jnp.dot(rows_in, w_query, preferred_element_type=jnp.float32).astype(jnp.bfloat16)
        query_heads = query.astype(jnp.float32).reshape(P_DEV, HEADS, HD)
        scores = jnp.einsum('phd,lhd->hpl', query_heads, key_heads) * scale
        probs = jax.nn.softmax(scores, axis=-1).astype(jnp.bfloat16)
        probs_f = probs.astype(jnp.float32)
        attended = jnp.einsum('hpl,lhd->phd', probs_f, value_heads).astype(jnp.bfloat16).reshape(P_DEV, D)
        mixed = rows_in.astype(jnp.float32) + jnp.dot(attended, w_out, preferred_element_type=jnp.float32)
        mean = lax.optimization_barrier(jnp.mean(mixed, axis=-1, keepdims=True))
        center = mixed - mean
        var = lax.optimization_barrier(jnp.mean(center * center, axis=-1, keepdims=True))
        rstd = lax.rsqrt(var + EPSILON)
        normal_rows = center * rstd
        normed = (normal_rows * gain).astype(jnp.bfloat16)
        hidden_pre = jnp.dot(normed, w_hidden, preferred_element_type=jnp.float32)
        activated = jax.nn.gelu(hidden_pre).astype(jnp.bfloat16)
        logit = jnp.dot(activated, w_logit, preferred_element_type=jnp.float32)
        d_logit = (jax.nn.sigmoid(logit) - label_rows.astype(jnp.float32)) * inv_root
        grad_w2 = jnp.dot(d_logit, activated.astype(jnp.float32))
        _, pull = jax.vjp(jax.nn.gelu, hidden_pre)
        d_hidden = pull(d_logit[:, None] * w_logit.astype(jnp.float32)[None, :])[0].astype(jnp.bfloat16)
        grad_w1 = jnp.dot(normed.T, d_hidden, preferred_element_type=jnp.float32)
        d_normed = jnp.dot(d_hidden, w_hidden.T, preferred_element_type=jnp.float32)
        grad_g = lax.optimization_barrier(jnp.sum(d_normed * normal_rows, axis=0))
        scaled = d_normed * gain
        d_mixed = rstd * (scaled - lax.optimization_barrier(jnp.mean(scaled, axis=-1, keepdims=True)) - normal_rows * lax.optimization_barrier(jnp.mean(scaled * normal_rows, axis=-1, keepdims=True)))
        d_mixed = d_mixed.astype(jnp.bfloat16)
        grad_wo = jnp.dot(attended.T, d_mixed, preferred_element_type=jnp.float32)
        d_attended = jnp.dot(d_mixed, w_out.T, preferred_element_type=jnp.float32).astype(jnp.bfloat16)
        d_att_heads = d_attended.astype(jnp.float32).reshape(P_DEV, HEADS, HD)
        att_heads = attended.astype(jnp.float32).reshape(P_DEV, HEADS, HD)
        d_probs = jnp.einsum('phd,lhd->hpl', d_att_heads, value_heads)
        delta = jnp.einsum('phd,phd->hp', d_att_heads, att_heads)
        d_scores = (probs_f * (d_probs - delta[:, :, None]) * scale).astype(jnp.bfloat16)
        d_scores_f = d_scores.astype(jnp.float32)
        d_query = jnp.einsum('hpl,lhd->phd', d_scores_f, key_heads).astype(jnp.bfloat16).reshape(P_DEV, D)
        grad_wq = jnp.dot(rows_in.T, d_query, preferred_element_type=jnp.float32)
        grad_k = jnp.einsum('hpl,phd->lhd', d_scores_f, query_heads).reshape(LAT, D)
        grad_v = jnp.einsum('hpl,phd->lhd', probs_f, d_att_heads).reshape(LAT, D)
        terms = (grad_wq, grad_wo, grad_w1, grad_w2, grad_g, grad_k, grad_v)
        return (tuple((c + t for c, t in zip(carry, terms))), None)
    start = (jnp.zeros((D, D), jnp.float32), jnp.zeros((D, D), jnp.float32), jnp.zeros((D, FF), jnp.float32), jnp.zeros((FF,), jnp.float32), jnp.zeros((D,), jnp.float32), jnp.zeros((LAT, D), jnp.float32), jnp.zeros((LAT, D), jnp.float32))
    totals, _ = lax.scan(step, start, (pool_blocks, index_blocks, label_blocks))
    grad_wq, grad_wo, grad_w1, grad_w2, grad_g, grad_k, grad_v = totals
    return (grad_wq, grad_wo, grad_w1, grad_w2, grad_g, grad_k, grad_v)
```

```python
import jax
import jax.numpy as jnp
from jax import lax
from jax.experimental import pallas as pl
from jax.experimental.pallas import tpu as pltpu
from jax.sharding import PartitionSpec as P

HD = 64
EPSILON = 1e-05
NX = 4
NC = 2
PIECES = 9
MESH = pl.DeviceIdType.MESH
F32 = jnp.float32
BF16 = jnp.bfloat16


def dot(a, b):
    return jnp.dot(a, b, preferred_element_type=F32)


def dot_nt(a, b):
    return lax.dot_general(a, b, (((1,), (1,)), ((), ())), preferred_element_type=F32)


class Links:
    def __init__(self, nz, ny, sems):
        self.nz, self.ny, self.sems, self.used = nz, ny, sems, 0
        p = lax.axis_index("pts")
        self.y = lax.axis_index("head")
        self.c = p % NC
        self.x = (p // NC) % NX
        self.z = p // (NC * NX)
        self.other = 1 - self.c
        self.ends = []

    def at(self, x=None, y=None, z=None, c=None):
        x = self.x if x is None else x
        y = self.y if y is None else y
        z = self.z if z is None else z
        c = self.c if c is None else c
        return (z * (NC * NX) + x * NC + c, y)

    def x_at(self, d):
        return self.at(x=(self.x + d) % NX)

    def y_at(self, d):
        return self.at(y=(self.y + d) % self.ny)

    def z_at(self, d):
        return self.at(z=(self.z + d) % self.nz)

    def sibling(self):
        return self.at(c=self.other)

    def take(self, count):
        first = self.used
        self.used += count
        return first

    def copy(self, src, dst, send, recv, device):
        return pltpu.make_async_remote_copy(
            src_ref=src,
            dst_ref=dst,
            send_sem=self.sems.at[send],
            recv_sem=self.sems.at[recv],
            device_id=device,
            device_id_type=MESH,
        )

    def send(self, src, dst, send, recv, device):
        copy = self.copy(src, dst, send, recv, device)
        copy.start()
        self.ends.append(copy.wait_send)

    def arrived(self, dst, recv):
        self.copy(dst, dst, recv, recv, self.sibling()).wait_recv()

    def finish(self):
        for end in self.ends:
            end()


class WeightSum:
    def __init__(self, net, refs, mirrored):
        self.net, self.mirrored = net, mirrored
        self.part, self.cr, self.xs, self.xr, self.zs, self.zr, self.full = refs
        nz = net.nz
        self.s_core, self.r_core = net.take(1), net.take(1)
        self.s_x, self.r_x = net.take(NX - 1), net.take(NX - 1)
        self.s_z, self.r_z = net.take(PIECES), net.take(nz - 1)
        self.s_gz, self.r_gz = net.take(nz - 1), net.take(PIECES)
        self.s_gx, self.r_gx = net.take(NX - 1), net.take(NX - 1)
        self.s_gc, self.r_gc = net.take(1), net.take(1)
        mine = (nz - 1 - net.z) if mirrored else net.z
        self.piece = (PIECES * mine + nz - 1) // nz
        self.reduces = (nz * self.piece) // PIECES == mine

    def owner(self, piece):
        spot = (self.net.nz * piece) // PIECES
        return self.net.nz - 1 - spot if self.mirrored else spot

    def put(self, c, x, block):
        block = block.astype(BF16)
        for j in range(PIECES):
            r, l = 16 * (j // 3), 128 * (j % 3)
            self.part[c, x, j] = block[r : r + 16, l : l + 128]

    def start(self):
        net = self.net
        net.send(self.part.at[net.other], self.cr, self.s_core, self.r_core, net.sibling())

    def to_x(self):
        net = self.net
        net.arrived(self.cr, self.r_core)
        self.xs[...] = (self.part[net.c].astype(F32) + self.cr[...].astype(F32)).astype(BF16)
        for d in range(1, NX):
            target = (net.x + d) % NX
            net.send(
                self.xs.at[target], self.xr.at[d - 1], self.s_x + d - 1, self.r_x + d - 1, net.x_at(d)
            )

    def to_z(self):
        net = self.net
        total = self.xs[net.x].astype(F32)
        for d in range(1, NX):
            net.arrived(self.xr.at[d - 1], self.r_x + d - 1)
            total += self.xr[d - 1].astype(F32)
        self.zs[...] = total.astype(BF16)
        for j in range(PIECES):
            way = (self.owner(j) - net.z + net.nz) % net.nz

            def copy(j=j, way=way):
                return net.copy(
                    self.zs.at[j],
                    self.zr.at[way - 1],
                    self.s_z + j,
                    self.r_z + way - 1,
                    net.at(z=self.owner(j)),
                )

            @pl.when(way != 0)
            def _(copy=copy):
                copy().start()

            @net.ends.append
            def _(copy=copy, way=way):
                @pl.when(way != 0)
                def _():
                    copy().wait_send()

    def back_z(self):
        net = self.net
        tile = self.full.at[net.c, net.x, self.piece]

        def copy(d):
            return net.copy(tile, tile, self.s_gz + d - 1, self.r_gz + self.piece, net.z_at(d))

        @pl.when(self.reduces)
        def _():
            total = self.zs[self.piece].astype(F32)
            for d in range(1, net.nz):
                net.arrived(self.zr.at[d - 1], self.r_z + d - 1)
                total += self.zr[d - 1].astype(F32)
            self.full[net.c, net.x, self.piece] = total.astype(BF16)
            for d in range(1, net.nz):
                copy(d).start()

        @net.ends.append
        def _():
            @pl.when(self.reduces)
            def _():
                for d in range(1, net.nz):
                    copy(d).wait_send()

    def back_x(self):
        net = self.net
        for j in range(PIECES):

            @pl.when(net.z != self.owner(j))
            def _(j=j):
                net.arrived(self.full.at[net.c, net.x, j], self.r_gz + j)

        mine = self.full.at[net.c, net.x]
        for d in range(1, NX):
            net.send(mine, mine, self.s_gx + d - 1, self.r_gx + d - 1, net.x_at(d))

    def back_core(self):
        net = self.net
        for d in range(1, NX):
            source = (net.x + NX - d) % NX
            net.arrived(self.full.at[net.c, source], self.r_gx + d - 1)
        mine = self.full.at[net.c]
        net.send(mine, mine, self.s_gc, self.r_gc, net.sibling())

    def end(self):
        net = self.net
        net.arrived(self.full.at[net.other], self.r_gc)

    def block(self, c, x):
        rows = []
        for r in range(3):
            rows.append(jnp.concatenate([self.full[c, x, 3 * r + l] for l in range(3)], axis=1))
        return jnp.concatenate(rows, axis=0)


def kernel(
    nz,
    ny,
    pool_ref,
    index_ref,
    label_ref,
    w_query_ref,
    kv_ref,
    w_out_ref,
    gain_ref,
    w_hidden_ref,
    w_logit_ref,
    owh_ref,
    owo_ref,
    owq_ref,
    small_ref,
    okv_ref,
    rows_buf,
    rows_in,
    wo_full,
    wh_full,
    wl_full,
    kvx,
    kv_buf,
    q_ref,
    probs,
    att_t,
    att_buf,
    normal_ref,
    normed_ref,
    act_ref,
    slope_ref,
    dh_ref,
    ws_part,
    ws_cr,
    ws_xs,
    ws_xr,
    ws_zs,
    ws_zr,
    ws_full,
    gkv,
    gkv_cr,
    gkv_xs,
    gkv_xr,
    gkv_zs,
    gkv_zr,
    gkv_sum,
    small_0,
    small_cr,
    small_x,
    small_z,
    sems,
):
    net = Links(nz, ny, sems)
    x, y, z, c, other = net.x, net.y, net.z, net.c, net.other
    points = rows_in.shape[0]
    half_z = nz // 2

    barrier = pltpu.get_barrier_semaphore()
    partners = [net.sibling()]
    partners += [net.x_at(d) for d in range(1, NX)]
    partners += [net.y_at(d) for d in range(1, ny)]
    partners += [net.z_at(d) for d in range(1, nz)]
    for device in partners:
        pl.semaphore_signal(barrier, inc=1, device_id=device, device_id_type=MESH)

    spots = lax.broadcasted_iota(jnp.int32, (points, pool_ref.shape[0]), 1)
    chosen = jnp.where(spots == index_ref[...], 1.0, 0.0).astype(BF16)
    rows_buf[y] = dot(chosen, pool_ref[...]).astype(BF16)
    wo_full[y] = w_out_ref[...]
    wh_full[y] = w_hidden_ref[...]
    wl_full[y] = w_logit_ref[...]
    pl.semaphore_wait(barrier, len(partners))

    hub = z % 2 == c
    s_kvx, r_kvx = net.take(1), net.take(1)
    s_kz, r_kz = net.take(nz - 1), net.take(half_z)
    s_kx, r_kx = net.take(NX - 1), net.take(NX - 1)
    s_kc, r_kc = net.take(NX), net.take(NX)
    kv_own = kv_buf.at[c, x, z // 2]

    def kvx_copy():
        return net.copy(kv_ref, kvx, s_kvx, r_kvx, net.sibling())

    def kz_copy(d):
        return net.copy(kv_own, kv_own, s_kz + d - 1, r_kz + z // 2, net.z_at(d))

    @pl.when(jnp.logical_not(hub))
    def _():
        kvx_copy().start()

    s_rows, r_rows = net.take(ny - 1), net.take(ny - 1)
    for d in range(1, ny):
        net.send(rows_buf.at[y], rows_buf.at[y], s_rows + d - 1, r_rows + d - 1, net.y_at(d))

    @pl.when(hub)
    def _():
        net.arrived(kvx, r_kvx)
        own, extra = kv_ref[...], kvx[...]
        low = jnp.where(c == 0, own, extra)
        high = jnp.where(c == 0, extra, own)
        kv_buf[c, x, z // 2] = jnp.concatenate([low, high], axis=0).astype(BF16)
        for d in range(1, nz):
            kz_copy(d).start()

    for d in range(1, ny):
        net.arrived(rows_buf.at[(y + ny - d) % ny], r_rows + d - 1)

    s_wo, r_wo = net.take(ny - 1), net.take(ny - 1)
    s_wh, r_wh = net.take(ny - 1), net.take(ny - 1)
    s_wl, r_wl = net.take(ny - 1), net.take(ny - 1)
    s_fo, r_fo = net.take(ny - 1), net.take(ny - 1)
    s_fh, r_fh = net.take(ny - 1), net.take(ny - 1)
    o_rows, h_rows = w_out_ref.shape[0] // 2, w_hidden_ref.shape[0] // 2

    def wo_half(owner, core):
        return wo_full.at[owner, pl.ds(core * o_rows, o_rows)]

    def wh_half(owner, core):
        return wh_full.at[owner, pl.ds(core * h_rows, h_rows)]

    for d in range(1, ny):
        net.send(wl_full.at[y], wl_full.at[y], s_wl + d - 1, r_wl + d - 1, net.y_at(d))
    for d in range(1, ny):
        net.send(wo_half(y, c), wo_half(y, c), s_wo + d - 1, r_wo + d - 1, net.y_at(d))
    for d in range(1, ny):
        net.send(wh_half(y, c), wh_half(y, c), s_wh + d - 1, r_wh + d - 1, net.y_at(d))

    rows_in[...] = jnp.concatenate([rows_buf[i] for i in range(ny)], axis=1)
    query = dot(rows_in[...], w_query_ref[...]).astype(BF16)
    q_ref[...] = query

    for i in range(half_z):

        @pl.when(jnp.logical_or(z % 2 != c, z // 2 != i))
        def _(i=i):
            net.arrived(kv_buf.at[c, x, i], r_kz + i)

    for d in range(1, NX):
        net.send(kv_buf.at[c, x], kv_buf.at[c, x], s_kx + d - 1, r_kx + d - 1, net.x_at(d))
    for d in range(NX):
        source = (x + NX - d) % NX
        block = kv_buf.at[c, source]
        if d:
            net.arrived(block, r_kx + d - 1)
        net.send(block, block, s_kc + d, r_kc + d, net.sibling())
    for d in range(NX):
        net.arrived(kv_buf.at[other, (x + NX - d) % NX], r_kc + d)

    columns = w_query_ref.shape[1]
    heads = columns // HD
    latents = 16 * half_z * NX * 2
    kv = kv_buf[...].reshape(latents, 2 * columns)
    kv_t = kv.T
    k_all, v_all = kv[:, :columns], kv[:, columns:]
    lane_head = lax.broadcasted_iota(jnp.int32, (points, columns), 1) // HD
    scale = HD ** (-0.5)
    log2e = 1.4426950408889634
    for h in range(heads):
        q_h = jnp.where(lane_head == h, query, jnp.zeros_like(query))
        raw = dot_nt(k_all, q_h)
        top = jnp.max(raw, axis=0, keepdims=True)
        e = jnp.exp2((raw - top) * (scale * log2e))
        p_h = (e * (1.0 / jnp.sum(e, axis=0, keepdims=True))).astype(BF16)
        probs[h] = p_h
        v_t = kv_t[columns + h * HD : columns + (h + 1) * HD]
        att_t[h * HD : (h + 1) * HD] = dot(v_t, p_h).astype(BF16)

    att_buf[y] = att_t[...].T
    s_att, r_att = net.take(ny - 1), net.take(ny - 1)
    for d in range(1, ny):
        net.send(att_buf.at[y], att_buf.at[y], s_att + d - 1, r_att + d - 1, net.y_at(d))

    for d in range(1, ny):
        source = (y + ny - d) % ny
        net.arrived(wo_half(source, c), r_wo + d - 1)
        net.send(wo_half(source, c), wo_half(source, c), s_fo + d - 1, r_fo + d - 1, net.sibling())
    for d in range(1, ny):
        source = (y + ny - d) % ny
        net.arrived(wh_half(source, c), r_wh + d - 1)
        net.send(wh_half(source, c), wh_half(source, c), s_fh + d - 1, r_fh + d - 1, net.sibling())
        net.arrived(wl_full.at[source], r_wl + d - 1)
    for d in range(1, ny):
        source = (y + ny - d) % ny
        net.arrived(wo_half(source, other), r_fo + d - 1)
        net.arrived(att_buf.at[source], r_att + d - 1)

    mixed = rows_in[...].astype(F32)
    for i in range(ny):
        mixed += dot(att_buf[i], wo_full[i])
    center = mixed - jnp.mean(mixed, axis=1, keepdims=True)
    rstd = lax.rsqrt(jnp.mean(center * center, axis=1, keepdims=True) + EPSILON)
    gain = gain_ref[...]
    normal = center * rstd
    normal_ref[...] = normal
    normed_ref[...] = (normal * gain).astype(BF16)

    for d in range(1, ny):
        net.arrived(wh_half((y + ny - d) % ny, other), r_fh + d - 1)

    root = 0.7978845608028654
    cubic = 0.044715
    logit = jnp.zeros((points, 1), F32)
    for i in range(ny):
        v = dot(normed_ref[...], wh_full[i])
        t = jnp.tanh(root * (v + cubic * (v * v * v)))
        act = (0.5 * v * (1.0 + t)).astype(BF16)
        act_ref[i] = act
        slope_ref[i] = 0.5 * (1.0 + t) + 0.5 * v * (1.0 - t * t) * (root * (1.0 + 3.0 * cubic * (v * v)))
        logit += jnp.sum(act.astype(F32) * wl_full[i], axis=1, keepdims=True)
    total_points = points * nz * NX * NC
    d_logit = (jax.nn.sigmoid(logit) - label_ref[...].astype(F32)) * total_points ** (-0.5)
    for i in range(ny):
        dh_ref[i] = (d_logit * wl_full[i] * slope_ref[i]).astype(BF16)
    grad_logit = jnp.sum(d_logit * act_ref[y].astype(F32), axis=0, keepdims=True)

    sums = []
    for i in range(4):
        refs = [r.at[i] for r in (ws_part, ws_cr, ws_xs, ws_xr, ws_zs, ws_zr, ws_full)]
        sums.append(WeightSum(net, refs, i % 2 == 1))
    hidden_1, hidden_2, outs, queries = sums

    normed_t = normed_ref[...].T
    depth = normed_t.shape[0] // 2
    for k, chunk in enumerate((hidden_1, hidden_2)):
        grad = dot(normed_t[k * depth : (k + 1) * depth], dh_ref[y])
        for cc in range(NC):
            for xx in range(NX):
                row = (cc * NX + xx) * 48
                chunk.put(cc, xx, grad[row : row + 48])
        chunk.start()

    d_normed = dot_nt(dh_ref[0], wh_full[0])
    for i in range(1, ny):
        d_normed += dot_nt(dh_ref[i], wh_full[i])
    normal = normal_ref[...]
    both = d_normed * normal
    grad_gain = jnp.sum(both, axis=0, keepdims=True)
    scaled = d_normed * gain
    d_mixed = rstd * (
        scaled
        - jnp.mean(scaled, axis=1, keepdims=True)
        - normal * jnp.mean(both * gain, axis=1, keepdims=True)
    )
    d_mixed = d_mixed.astype(BF16)

    hidden_1.to_x()
    hidden_2.to_x()

    lines = [grad_logit[:, 128 * i : 128 * (i + 1)] for i in range(3)]
    lines += [grad_gain[:, 128 * i : 128 * (i + 1)] for i in range(6)]
    lines += [jnp.zeros((1, 128), F32)]
    for i, line in enumerate(lines):
        small_0[i // 5, i % 5] = line
    s_sc, r_sc = net.take(1), net.take(1)
    s_sx, r_sx = net.take(NX - 1), net.take(NX - 1)
    s_sz, r_sz = net.take(nz - 1), net.take(nz - 1)
    s_sf, r_sf = net.take(1), net.take(1)
    net.send(small_0.at[other], small_cr, s_sc, r_sc, net.sibling())

    def block_rows(chunk, grad):
        for cc in range(NC):
            for xx in range(NX):
                chunk.put(cc, xx, grad[xx * 48 : xx * 48 + 48, cc * 384 : cc * 384 + 384])

    block_rows(outs, dot(att_t[...], d_mixed))
    outs.start()
    w_out = w_out_ref[...]
    d_att = dot_nt(d_mixed, w_out).astype(BF16)
    d_att_t = dot_nt(w_out, d_mixed).astype(BF16)

    net.arrived(small_cr, r_sc)
    small_x[x] = small_0[c] + small_cr[...]
    for d in range(1, NX):
        net.send(small_x.at[x], small_x.at[x], s_sx + d - 1, r_sx + d - 1, net.x_at(d))

    hidden_1.to_z()
    hidden_2.to_z()
    outs.to_x()

    query = q_ref[...]
    kv = kv_buf[...].reshape(latents, 2 * columns)
    kv_t = kv.T
    v_all = kv[:, columns:]
    grad_k = jnp.zeros((latents, columns), F32)
    grad_v = jnp.zeros((latents, columns), F32)
    d_query = []
    for h in range(heads):
        rows = slice(h * HD, (h + 1) * HD)
        p_h = probs[h]
        d_att_h = jnp.where(lane_head == h, d_att, jnp.zeros_like(d_att))
        q_h = jnp.where(lane_head == h, query, jnp.zeros_like(query))
        delta = jnp.sum(d_att_t[rows].astype(F32) * att_t[rows].astype(F32), axis=0, keepdims=True)
        d_probs = dot_nt(v_all, d_att_h)
        d_scores = (p_h.astype(F32) * (d_probs - delta) * scale).astype(BF16)
        d_query.append(dot(kv_t[rows], d_scores).astype(BF16))
        grad_k += dot(d_scores, q_h)
        grad_v += dot(p_h, d_att_h)
    block_rows(queries, dot(jnp.concatenate(d_query, axis=0), rows_in[...]))
    queries.start()
    grads = jnp.concatenate([grad_k, grad_v], axis=1).astype(BF16)
    gkv[...] = grads.reshape(gkv.shape)
    s_gc, r_gc = net.take(1), net.take(1)
    s_gx, r_gx = net.take(NX - 1), net.take(NX - 1)
    s_gz, r_gz = net.take(half_z), net.take(nz - 1)
    s_gf, r_gf = net.take(1), net.take(1)
    net.send(gkv.at[other], gkv_cr, s_gc, r_gc, net.sibling())

    queries.to_x()
    hidden_1.back_z()
    hidden_2.back_z()
    outs.to_z()

    for d in range(1, NX):
        net.arrived(small_x.at[(x + NX - d) % NX], r_sx + d - 1)
    line = small_x[0]
    for i in range(1, NX):
        line += small_x[i]
    small_z[z] = line
    for d in range(1, nz):
        net.send(small_z.at[z], small_z.at[z], s_sz + d - 1, r_sz + d - 1, net.z_at(d))

    net.arrived(gkv_cr, r_gc)
    gkv_xs[...] = (gkv[c].astype(F32) + gkv_cr[...].astype(F32)).astype(BF16)
    for d in range(1, NX):
        net.send(
            gkv_xs.at[(x + d) % NX], gkv_xr.at[d - 1], s_gx + d - 1, r_gx + d - 1, net.x_at(d)
        )

    queries.to_z()
    hidden_1.back_x()
    hidden_2.back_x()
    outs.back_z()

    total = gkv_xs[x].astype(F32)
    for d in range(1, NX):
        net.arrived(gkv_xr.at[d - 1], r_gx + d - 1)
        total += gkv_xr[d - 1].astype(F32)
    gkv_zs[...] = total.astype(BF16)
    for i in range(half_z):
        target = 2 * i + c
        way = (target - z + nz) % nz

        def copy(i=i, target=target, way=way):
            return net.copy(
                gkv_zs.at[i], gkv_zr.at[way - 1], s_gz + i, r_gz + way - 1, net.at(z=target)
            )

        @pl.when(way != 0)
        def _(copy=copy):
            copy().start()

        @net.ends.append
        def _(copy=copy, way=way):
            @pl.when(way != 0)
            def _():
                copy().wait_send()

    queries.back_z()
    hidden_1.back_core()
    hidden_2.back_core()
    outs.back_x()

    for d in range(1, nz):
        net.arrived(small_z.at[(z + nz - d) % nz], r_sz + d - 1)
    line = small_z[0]
    for i in range(1, nz):
        line += small_z[i]
    small_ref[c] = line
    net.send(small_ref.at[c], small_ref.at[c], s_sf, r_sf, net.sibling())

    queries.back_x()

    def gf_copy():
        return net.copy(
            gkv_sum.at[other], okv_ref, s_gf, r_gf, net.sibling()
        )

    @pl.when(hub)
    def _():
        total = gkv_zs[z // 2].astype(F32)
        for d in range(1, nz):
            net.arrived(gkv_zr.at[d - 1], r_gz + d - 1)
            total += gkv_zr[d - 1].astype(F32)
        gkv_sum[...] = total.reshape(gkv_sum.shape)
        gf_copy().start()
        okv_ref[...] = gkv_sum[c]

    outs.back_core()
    queries.back_core()

    for chunk, first in ((hidden_1, 0), (hidden_2, depth)):
        chunk.end()
        for cc in range(NC):
            for xx in range(NX):
                row = first + (cc * NX + xx) * 48
                owh_ref[row : row + 48, :] = chunk.block(cc, xx)
    for chunk, ref in ((outs, owo_ref), (queries, owq_ref)):
        chunk.end()
        for cc in range(NC):
            for xx in range(NX):
                ref[xx * 48 : xx * 48 + 48, cc * 384 : cc * 384 + 384] = chunk.block(cc, xx)

    @pl.when(jnp.logical_not(hub))
    def _():
        net.arrived(okv_ref, r_gf)

    net.arrived(small_ref.at[other], r_sf)

    @pl.when(hub)
    def _():
        for d in range(1, nz):
            kz_copy(d).wait_send()
        gf_copy().wait_send()

    @pl.when(jnp.logical_not(hub))
    def _():
        kvx_copy().wait_send()

    net.finish()


def solution(mesh):
    nz = mesh.shape["pts"] // (NX * NC)
    ny = mesh.shape["head"]
    half_z = nz // 2

    def on_device(pool, index, labels, w_query, keys, values, w_out, out_gain, w_hidden, w_logit):
        points, columns = index.shape[0], keys.shape[1]
        width, hidden = w_hidden.shape
        latents = keys.shape[0] * nz * NX * NC
        heads = columns // HD
        kv = jnp.concatenate([keys, values], axis=1).astype(F32)
        vmem = pltpu.VMEM
        tile = (16, 128)
        wide = (16, 2 * columns)
        scratch = [
            vmem((ny, points, columns), BF16),
            vmem((points, width), BF16),
            vmem((ny, columns, width), BF16),
            vmem((ny, width, hidden), BF16),
            vmem((ny, 1, hidden), F32),
            vmem((8, 2 * columns), F32),
            vmem((2, NX, half_z) + wide, BF16),
            vmem((points, columns), BF16),
            vmem((heads, latents, points), BF16),
            vmem((columns, points), BF16),
            vmem((ny, points, columns), BF16),
            vmem((points, width), F32),
            vmem((points, width), BF16),
            vmem((ny, points, hidden), BF16),
            vmem((ny, points, hidden), F32),
            vmem((ny, points, hidden), BF16),
            vmem((4, NC, NX, PIECES) + tile, BF16),
            vmem((4, NX, PIECES) + tile, BF16),
            vmem((4, NX, PIECES) + tile, BF16),
            vmem((4, NX - 1, PIECES) + tile, BF16),
            vmem((4, PIECES) + tile, BF16),
            vmem((4, nz - 1) + tile, BF16),
            vmem((4, NC, NX, PIECES) + tile, BF16),
            vmem((2, NX, half_z) + wide, BF16),
            vmem((NX, half_z) + wide, BF16),
            vmem((NX, half_z) + wide, BF16),
            vmem((NX - 1, half_z) + wide, BF16),
            vmem((half_z,) + wide, BF16),
            vmem((nz - 1,) + wide, BF16),
            vmem((2, 8, 2 * columns), F32),
            vmem((NC, 5, 1, 128), F32),
            vmem((5, 1, 128), F32),
            vmem((NX, 5, 1, 128), F32),
            vmem((nz, 5, 1, 128), F32),
            pltpu.SemaphoreType.DMA((512,)),
        ]
        shapes = [
            jax.ShapeDtypeStruct((width, hidden), BF16),
            jax.ShapeDtypeStruct((columns, width), BF16),
            jax.ShapeDtypeStruct((columns, width), BF16),
            jax.ShapeDtypeStruct((NC, 5, 1, 128), F32),
            jax.ShapeDtypeStruct((8, 2 * columns), F32),
        ]
        whole = pl.BlockSpec(memory_space=pltpu.VMEM)
        grad_wh, grad_wo, grad_wq, small, grad_kv = pl.pallas_call(
            lambda *refs: kernel(nz, ny, *refs),
            out_shape=shapes,
            in_specs=[whole] * 9,
            out_specs=[whole] * 5,
            scratch_shapes=scratch,
            compiler_params=pltpu.CompilerParams(
                collective_id=0, has_side_effects=True, vmem_limit_bytes=60 * 1024 * 1024
            ),
        )(
            pool,
            index.reshape(points, 1),
            labels.reshape(points, 1),
            w_query,
            kv,
            w_out,
            out_gain.astype(F32).reshape(1, width),
            w_hidden,
            w_logit.astype(F32).reshape(1, hidden),
        )
        small = small.reshape(-1)
        return (
            grad_wq.T.astype(F32),
            grad_wo.astype(F32),
            grad_wh.astype(F32),
            small[:hidden],
            small[hidden : hidden + width],
            grad_kv[:, :columns],
            grad_kv[:, columns:],
        )

    return jax.shard_map(
        on_device,
        mesh=mesh,
        in_specs=(
            P("pts", "head"),
            P("pts"),
            P("pts"),
            P(None, "head"),
            P("pts", "head"),
            P("pts", "head"),
            P("head", None),
            P(),
            P(None, "head"),
            P("head"),
        ),
        out_specs=(
            P(None, "head"),
            P("head", None),
            P(None, "head"),
            P("head"),
            P(),
            P("pts", "head"),
            P("pts", "head"),
        ),
        check_vma=False,
    )
```

```python
import jax
import jax.numpy as jnp
from jax import lax
from jax.experimental import pallas as pl
from jax.experimental.pallas import tpu as pltpu
from jax.sharding import PartitionSpec as P

HD = 64
EPSILON = 1e-05
NX = 4
NC = 2
PIECES = 9
SEMAPHORES = 112
MESH = pl.DeviceIdType.MESH
F32 = jnp.float32
BF16 = jnp.bfloat16


def dot(a, b):
    return jnp.dot(a, b, preferred_element_type=F32)


def dot_nt(a, b):
    return lax.dot_general(a, b, (((1,), (1,)), ((), ())), preferred_element_type=F32)


def far_first(n):
    return sorted(range(1, n), key=lambda d: -min(d, n - d))


def packed(block):
    half = block.shape[0] // 2
    return block[:, :128], jnp.concatenate([block[:half, 128:], block[half:, 128:]], axis=1)


def folded(block):
    half = block.shape[0] // 2
    return jnp.concatenate([block[:half], block[half:]], axis=1)


def unfolded(block):
    return jnp.concatenate([block[:, :64], block[:, 64:]], axis=0)


def unpacked(wide, narrow):
    return jnp.concatenate([wide, jnp.concatenate([narrow[:, :64], narrow[:, 64:]], axis=0)], axis=1)


class Links:
    def __init__(self, nz, ny, sems):
        self.nz, self.ny, self.sems, self.used = nz, ny, sems, 0
        p = lax.axis_index("pts")
        self.y = lax.axis_index("head")
        self.c = p % NC
        self.x = (p // NC) % NX
        self.z = p // (NC * NX)
        self.other = 1 - self.c
        self.ends = []

    def at(self, x=None, y=None, z=None, c=None):
        x = self.x if x is None else x
        y = self.y if y is None else y
        z = self.z if z is None else z
        c = self.c if c is None else c
        return (z * (NC * NX) + x * NC + c, y)

    def x_at(self, d):
        return self.at(x=(self.x + d) % NX)

    def y_at(self, d):
        return self.at(y=(self.y + d) % self.ny)

    def z_at(self, d):
        return self.at(z=(self.z + d) % self.nz)

    def sibling(self):
        return self.at(c=self.other)

    def take(self, count):
        first = self.used
        self.used += count
        return first

    def copy(self, src, dst, send, recv, device):
        return pltpu.make_async_remote_copy(
            src_ref=src,
            dst_ref=dst,
            send_sem=self.sems.at[send],
            recv_sem=self.sems.at[recv if isinstance(recv, int) else sum(recv)],
            device_id=device,
            device_id_type=MESH,
        )

    def pair(self):
        return self.take(1), self.take(1)

    def send(self, src, dst, pair, device):
        self.copy(src, dst, pair[0], pair[1], device).start()

    def arrived(self, total, recv):
        self.copy(total, total, 0, recv, self.sibling()).wait_recv()

    def sent(self, total, pair):
        self.copy(total, total, pair[0], 0, self.sibling()).wait_send()

    def later(self, total, pair):
        self.ends.append(lambda: self.sent(total, pair))

    def finish(self):
        for end in self.ends:
            end()


class WeightSum:
    def __init__(self, net, refs, mirrored):
        self.net, self.mirrored = net, mirrored
        self.part, self.cr, self.xs, self.xr, self.zs, self.zr, self.full = refs
        nz = net.nz
        self.core, self.x, self.z = net.pair(), net.pair(), net.pair()
        self.gz, self.gx, self.gc = net.pair(), net.pair(), net.pair()
        self.piece, self.reduces = self.role(net.z)

    def role(self, z):
        nz = self.net.nz
        spot = (nz - 1 - z) if self.mirrored else z
        piece = (PIECES * spot + nz - 1) // nz
        return jnp.minimum(piece, PIECES - 1), (nz * piece) // PIECES == spot

    def owner(self, piece):
        spot = (self.net.nz * piece) // PIECES
        return self.net.nz - 1 - spot if self.mirrored else spot

    def put(self, c, x, block):
        block = block.astype(BF16)
        for j in range(PIECES):
            r, l = 16 * (j // 3), 128 * (j % 3)
            self.part[c, x, j] = block[r : r + 16, l : l + 128]

    def start(self):
        net = self.net
        net.send(self.part.at[net.other], self.cr, self.core, net.sibling())
        net.later(self.cr, self.core)

    def to_x(self):
        net = self.net
        net.arrived(self.cr, self.core[1])
        self.xs[...] = (self.part[net.c].astype(F32) + self.cr[...].astype(F32)).astype(BF16)
        for d in far_first(NX):
            target = (net.x + d) % NX
            net.send(self.xs.at[target], self.xr.at[d - 1], self.x, net.x_at(d))
        net.later(self.xr, self.x)

    def to_z(self):
        net = self.net
        net.arrived(self.xr, self.x[1])
        total = self.xs[net.x].astype(F32)
        for d in range(1, NX):
            total += self.xr[d - 1].astype(F32)
        self.zs[...] = total.astype(BF16)
        for d in far_first(net.nz):
            spot = (net.z + d) % net.nz
            piece, reduces = self.role(spot)

            @pl.when(reduces)
            def _(d=d, piece=piece, spot=spot):
                net.send(self.zs.at[piece], self.zr.at[d - 1], self.z, net.at(z=spot))

        @net.ends.append
        def _():
            self.pieces(lambda total: net.sent(total, self.z))

    def pieces(self, wait):
        @pl.when(self.reduces)
        def _():
            wait(self.zs.at[pl.ds(0, PIECES - 1)])

        @pl.when(jnp.logical_not(self.reduces))
        def _():
            wait(self.zs)

    def back_z(self):
        net = self.net
        tile = self.full.at[net.c, net.x, self.piece]

        @pl.when(self.reduces)
        def _():
            net.arrived(self.zr, self.z[1])
            total = self.zs[self.piece].astype(F32)
            for d in range(1, net.nz):
                total += self.zr[d - 1].astype(F32)
            self.full[net.c, net.x, self.piece] = total.astype(BF16)
            for d in far_first(net.nz):
                net.send(tile, tile, self.gz, net.z_at(d))

        @net.ends.append
        def _():
            @pl.when(self.reduces)
            def _():
                net.sent(self.zr, self.gz)

    def back_x(self):
        net = self.net
        self.pieces(lambda total: net.arrived(total, self.gz[1]))
        mine = self.full.at[net.c, net.x]
        for d in far_first(NX):
            net.send(mine, mine, self.gx, net.x_at(d))
        net.later(self.xr, self.gx)

    def back_core(self):
        net = self.net
        net.arrived(self.xr, self.gx[1])
        mine = self.full.at[net.c]
        net.send(mine, mine, self.gc, net.sibling())
        net.later(mine, self.gc)

    def end(self):
        net = self.net
        net.arrived(self.full.at[net.other], self.gc[1])


def kernel(
    nz,
    ny,
    pool_hbm,
    index_hbm,
    label_hbm,
    gain_hbm,
    w_logit_hbm,
    w_query_hbm,
    keys_hbm,
    values_hbm,
    w_out_hbm,
    w_hidden_hbm,
    ws_hbm,
    small_hbm,
    okv_hbm,
    ws_full,
    small_ref,
    okv_ref,
    pool,
    index,
    label_ref,
    gain_ref,
    w_logit,
    w_query,
    keys,
    values,
    rows_wide,
    rows_narrow,
    rows_in,
    wo_full,
    wh_full,
    wl_full,
    kv_own,
    kvx,
    kv_buf,
    q_ref,
    probs,
    att_t,
    att_buf,
    kv_t_ref,
    ds_ref,
    normal_ref,
    normed_ref,
    act_ref,
    slope_ref,
    dh_ref,
    ws_part,
    ws_cr,
    ws_xs,
    ws_xr,
    ws_zs,
    ws_zr,
    gkv,
    gkv_cr,
    gkv_xs,
    gkv_xr,
    gkv_zs,
    gkv_zr,
    gkv_sum,
    small_0,
    small_cr,
    small_x,
    small_z,
    local,
    sems,
):
    net = Links(nz, ny, sems)
    x, y, z, c, other = net.x, net.y, net.z, net.c, net.other
    points, width = rows_in.shape
    half_z = nz // 2
    hidden = wh_full.shape[2]

    barrier = pltpu.get_barrier_semaphore()
    partners = [net.sibling()]
    partners += [net.x_at(d) for d in range(1, NX)]
    partners += [net.y_at(d) for d in range(1, ny)]
    partners += [net.z_at(d) for d in far_first(nz)]
    for device in partners:
        pl.semaphore_signal(barrier, inc=1, device_id=device, device_id_type=MESH)

    loads = [
        pltpu.make_async_copy(source, target, local.at[i])
        for i, (source, target) in enumerate(
            (
                (keys_hbm, keys),
                (values_hbm, values),
                (index_hbm, index),
                (pool_hbm, pool),
                (w_out_hbm, wo_full.at[y]),
                (w_hidden_hbm, wh_full.at[y]),
                (w_query_hbm, w_query),
                (label_hbm, label_ref),
                (gain_hbm, gain_ref),
                (w_logit_hbm, w_logit),
            )
        )
    ]
    for load in loads:
        load.start()
    loads[0].wait()
    loads[1].wait()
    kv_own[...] = jnp.concatenate([keys[...].astype(F32), values[...].astype(F32)], axis=1)
    pl.semaphore_wait(barrier, len(partners))

    hub = z % 2 == c
    kvx_pair, kx_pair, kc_pair = net.pair(), net.pair(), net.pair()
    s_kz, r_kz = net.take(1), net.take(half_z)
    kv_tile = kv_buf.at[c, x, z // 2]

    @pl.when(jnp.logical_not(hub))
    def _():
        net.send(kv_own, kvx, kvx_pair, net.sibling())

    loads[2].wait()
    loads[3].wait()
    spots = lax.broadcasted_iota(jnp.int32, (pool.shape[1], points), 0)
    chosen = jnp.where(spots == index[...].reshape(1, points), 1.0, 0.0).astype(BF16)
    picked = dot(pool[...], chosen).T.astype(BF16)
    wide, narrow = packed(picked)
    rows_wide[y] = wide
    rows_narrow[y] = narrow

    wide_pair, narrow_pair = net.pair(), net.pair()
    for d in far_first(ny):
        net.send(rows_wide.at[y], rows_wide.at[y], wide_pair, net.y_at(d))
        net.send(rows_narrow.at[y], rows_narrow.at[y], narrow_pair, net.y_at(d))
    others = pl.ds(0, ny - 1)
    net.later(rows_wide.at[others], wide_pair)
    net.later(rows_narrow.at[others], narrow_pair)

    @pl.when(hub)
    def _():
        net.arrived(kvx, kvx_pair[1])
        own, extra = kv_own[...], kvx[...]
        low = jnp.where(c == 0, own, extra)
        high = jnp.where(c == 0, extra, own)
        kv_buf[c, x, z // 2] = jnp.concatenate([low, high], axis=0).astype(BF16)
        for d in far_first(nz):
            net.send(kv_tile, kv_tile, (s_kz, (r_kz, z // 2)), net.z_at(d))

    @net.ends.append
    def _():
        @pl.when(hub)
        def _():
            net.sent(gkv_zr, (s_kz, 0))

        @pl.when(jnp.logical_not(hub))
        def _():
            net.sent(kv_own, kvx_pair)

    wo_pair, near_pair, far_pair, wl_pair = net.pair(), net.pair(), net.pair(), net.pair()
    wx_pair, fo_pair, fn_pair, ff_pair = net.pair(), net.pair(), net.pair(), net.pair()
    o_rows, h_rows = wo_full.shape[1] // 2, wh_full.shape[1] // 2
    x_rows = h_rows // NX
    far = ny // 2

    def wo_half(owner, core):
        return wo_full.at[owner, pl.ds(core * o_rows, o_rows)]

    def wh_half(owner, core):
        return wh_full.at[owner, pl.ds(core * h_rows, h_rows)]

    def wh_part(owner, core, part):
        return wh_full.at[owner, pl.ds(core * h_rows + part * x_rows, x_rows)]

    def wo_bytes(count):
        return wo_full.at[pl.ds(0, count), pl.ds(0, o_rows)]

    def wh_bytes(count):
        return wh_full.at[pl.ds(0, count), pl.ds(0, h_rows)]

    loads[4].wait()
    for d in far_first(ny):
        net.send(wo_half(y, c), wo_half(y, c), wo_pair, net.y_at(d))
    net.later(wo_bytes(ny - 1), wo_pair)
    loads[5].wait()
    loads[9].wait()
    wl_full[y] = w_logit[...].astype(F32).reshape(1, hidden)
    for d in far_first(ny):
        if d == far:
            net.send(wh_part(y, c, x), wh_part(y, c, x), far_pair, net.y_at(d))
        else:
            net.send(wh_half(y, c), wh_half(y, c), near_pair, net.y_at(d))
        net.send(wl_full.at[y], wl_full.at[y], wl_pair, net.y_at(d))
    net.later(wh_part(0, 0, 0), far_pair)
    net.later(wh_bytes(ny - 2), near_pair)
    net.later(wl_full.at[others], wl_pair)

    side = jnp.where(jnp.logical_and(z % 2 == 0, c == 1), half_z - 1, 1)
    blocks = []
    for k in range(half_z):
        away = (k + 1) // 2
        step = away * side if k % 2 else (half_z - away) * side
        block = (z // 2 + step) % half_z
        blocks.append(block)
        tile = kv_buf.at[c, x, block]
        if k:
            net.arrived(tile, (r_kz, block))
        else:

            @pl.when(jnp.logical_not(hub))
            def _(tile=tile, block=block):
                net.arrived(tile, (r_kz, block))

        for d in far_first(NX):
            net.send(tile, tile, kx_pair, net.x_at(d))
    net.later(gkv_xr, kx_pair)
    net.arrived(rows_wide.at[others], wide_pair[1])
    net.arrived(rows_narrow.at[others], narrow_pair[1])
    rows_in[...] = jnp.concatenate(
        [unpacked(rows_wide[i], rows_narrow[i]) for i in range(ny)], axis=1
    )
    loads[6].wait()
    query = dot_nt(rows_in[...], w_query[...]).astype(BF16)
    q_ref[...] = query
    own = kv_buf.at[c, x]
    net.send(own, own, kc_pair, net.sibling())
    net.arrived(gkv_xr, kx_pair[1])
    for d in range(1, NX):
        block = kv_buf.at[c, (x + NX - d) % NX]
        net.send(block, block, kc_pair, net.sibling())
    net.later(gkv_xs, kc_pair)
    net.arrived(gkv_xs, kc_pair[1])

    columns = w_query.shape[0]
    heads = columns // HD
    latents = 16 * half_z * NX * 2
    kv = kv_buf[...].reshape(latents, 2 * columns)
    kv_t_ref[...] = kv.T
    k_all, v_all = kv[:, :columns], kv[:, columns:]
    att_pair = net.pair()
    lane_head = lax.broadcasted_iota(jnp.int32, (points, columns), 1) // HD
    scale = HD ** (-0.5)
    log2e = 1.4426950408889634
    for h in range(heads):
        q_h = jnp.where(lane_head == h, query, jnp.zeros_like(query))
        raw = dot_nt(k_all, q_h)
        top = jnp.max(raw, axis=0, keepdims=True)
        e = jnp.exp2((raw - top) * (scale * log2e))
        p_h = (e * (1.0 / jnp.sum(e, axis=0, keepdims=True))).astype(BF16)
        probs[h] = p_h
        v_t = kv_t_ref[columns + h * HD : columns + (h + 1) * HD]
        att_h = dot(v_t, p_h).astype(BF16)
        att_t[h * HD : (h + 1) * HD] = att_h
        att_buf[y, h] = folded(att_h.T)
        for d in far_first(ny):
            net.send(att_buf.at[y, h], att_buf.at[y, h], att_pair, net.y_at(d))

    net.later(att_buf.at[others], att_pair)
    far_y = (y + ny - far) % ny
    net.arrived(wo_bytes(ny - 1), wo_pair[1])
    for d in range(1, ny):
        block = wo_half((y + ny - d) % ny, c)
        net.send(block, block, fo_pair, net.sibling())
    net.later(wo_bytes(ny - 1), fo_pair)
    net.arrived(wh_part(0, 0, 0), far_pair[1])
    for d in far_first(NX):
        net.send(wh_part(far_y, c, x), wh_part(far_y, c, x), wx_pair, net.x_at(d))
    three = wh_full.at[0, pl.ds(0, (NX - 1) * x_rows)]
    net.later(three, wx_pair)
    net.arrived(wl_full.at[others], wl_pair[1])
    net.arrived(wh_bytes(ny - 2), near_pair[1])
    for d in range(1, ny):
        if d != far:
            block = wh_half((y + ny - d) % ny, c)
            net.send(block, block, fn_pair, net.sibling())
    net.later(wh_bytes(ny - 2), fn_pair)
    net.arrived(three, wx_pair[1])
    net.send(wh_half(far_y, c), wh_half(far_y, c), ff_pair, net.sibling())
    net.later(wh_half(0, 0), ff_pair)
    net.arrived(wo_bytes(ny - 1), fo_pair[1])
    net.arrived(att_buf.at[others], att_pair[1])

    attended = jnp.concatenate(
        [unfolded(att_buf[i, h]) for i in range(ny) for h in range(heads)], axis=1
    )
    mixed = rows_in[...].astype(F32) + dot(attended, wo_full[...].reshape(width, width))
    center = mixed - jnp.mean(mixed, axis=1, keepdims=True)
    rstd = lax.rsqrt(jnp.mean(center * center, axis=1, keepdims=True) + EPSILON)
    loads[8].wait()
    gain = gain_ref[...].astype(F32).reshape(1, width)
    normal = center * rstd
    normal_ref[...] = normal
    normed_ref[...] = (normal * gain).astype(BF16)

    net.arrived(wh_bytes(ny - 2), fn_pair[1])
    net.arrived(wh_half(0, 0), ff_pair[1])

    root = 0.7978845608028654
    cubic = 0.044715
    logit = jnp.zeros((points, 1), F32)
    for i in range(ny):
        v = dot(normed_ref[...], wh_full[i])
        t = jnp.tanh(root * (v + cubic * (v * v * v)))
        act = (0.5 * v * (1.0 + t)).astype(BF16)
        act_ref[i] = act
        slope_ref[i] = 0.5 * (1.0 + t) + 0.5 * v * (1.0 - t * t) * (root * (1.0 + 3.0 * cubic * (v * v)))
        logit += jnp.sum(act.astype(F32) * wl_full[i], axis=1, keepdims=True)
    total_points = points * nz * NX * NC
    loads[7].wait()
    label = label_ref[...].astype(F32).reshape(1, points)
    label = jnp.broadcast_to(label, (8, points)).T[:, 0:1]
    d_logit = (jax.nn.sigmoid(logit) - label) * total_points ** (-0.5)
    for i in range(ny):
        dh_ref[i] = (d_logit * wl_full[i] * slope_ref[i]).astype(BF16)

    sums = []
    for i in range(4):
        refs = [r.at[i] for r in (ws_part, ws_cr, ws_xs, ws_xr, ws_zs, ws_zr, ws_full)]
        sums.append(WeightSum(net, refs, i % 2 == 1))
    hidden_1, hidden_2, outs, queries = sums

    normed_t = normed_ref[...].T
    depth = normed_t.shape[0] // 2
    for k, chunk in enumerate((hidden_1, hidden_2)):
        grad = dot(normed_t[k * depth : (k + 1) * depth], dh_ref[y])
        for cc in range(NC):
            for xx in range(NX):
                row = (cc * NX + xx) * 48
                chunk.put(cc, xx, grad[row : row + 48])
        chunk.start()
    grad_logit = jnp.sum(d_logit * act_ref[y].astype(F32), axis=0, keepdims=True)

    d_normed = dot_nt(dh_ref[0], wh_full[0])
    for i in range(1, ny):
        d_normed += dot_nt(dh_ref[i], wh_full[i])
    normal = normal_ref[...]
    both = d_normed * normal
    grad_gain = jnp.sum(both, axis=0, keepdims=True)
    scaled = d_normed * gain
    d_mixed = rstd * (
        scaled
        - jnp.mean(scaled, axis=1, keepdims=True)
        - normal * jnp.mean(both * gain, axis=1, keepdims=True)
    )
    d_mixed = d_mixed.astype(BF16)

    hidden_1.to_x()
    hidden_2.to_x()

    lines = [grad_logit[:, 128 * i : 128 * (i + 1)] for i in range(3)]
    lines += [grad_gain[:, 128 * i : 128 * (i + 1)] for i in range(6)]
    lines += [jnp.zeros((1, 128), F32)]
    for i, line in enumerate(lines):
        small_0[i // 5, i % 5] = line
    sc_pair, sx_pair, sz_pair, sf_pair = net.pair(), net.pair(), net.pair(), net.pair()
    net.send(small_0.at[other], small_cr, sc_pair, net.sibling())
    net.later(small_cr, sc_pair)

    def block_rows(chunk, grad):
        for cc in range(NC):
            for xx in range(NX):
                chunk.put(cc, xx, grad[xx * 48 : xx * 48 + 48, cc * 384 : cc * 384 + 384])

    w_out = wo_full[y]
    d_att = dot_nt(d_mixed, w_out).astype(BF16)
    d_att_t = dot_nt(w_out, d_mixed).astype(BF16)

    query = q_ref[...]
    v_all = kv_buf[...].reshape(latents, 2 * columns)[:, columns:]
    d_query = []
    for h in range(heads):
        rows = slice(h * HD, (h + 1) * HD)
        d_att_h = jnp.where(lane_head == h, d_att, jnp.zeros_like(d_att))
        delta = jnp.sum(d_att_t[rows].astype(F32) * att_t[rows].astype(F32), axis=0, keepdims=True)
        d_probs = dot_nt(v_all, d_att_h)
        d_scores = (probs[h].astype(F32) * (d_probs - delta) * scale).astype(BF16)
        ds_ref[h] = d_scores
        d_query.append(dot(kv_t_ref[rows], d_scores).astype(BF16))
    block_rows(queries, dot(jnp.concatenate(d_query, axis=0), rows_in[...]))
    queries.start()
    hidden_1.to_z()
    hidden_2.to_z()

    grad_k = jnp.zeros((latents, columns), F32)
    grad_v = jnp.zeros((latents, columns), F32)
    for h in range(heads):
        d_att_h = jnp.where(lane_head == h, d_att, jnp.zeros_like(d_att))
        q_h = jnp.where(lane_head == h, query, jnp.zeros_like(query))
        grad_k += dot(ds_ref[h], q_h)
        grad_v += dot(probs[h], d_att_h)
        if h == 0:
            queries.to_x()
    grads = jnp.concatenate([grad_k, grad_v], axis=1).astype(BF16)
    gkv[...] = grads.reshape(gkv.shape)
    gc_pair, gx_pair, gz_pair, gf_pair = net.pair(), net.pair(), net.pair(), net.pair()
    net.send(gkv.at[other], gkv_cr, gc_pair, net.sibling())
    net.later(gkv_cr, gc_pair)

    block_rows(outs, dot(att_t[...], d_mixed))
    outs.start()
    net.arrived(small_cr, sc_pair[1])
    small_x[x] = small_0[c] + small_cr[...]
    for d in far_first(NX):
        net.send(small_x.at[x], small_x.at[x], sx_pair, net.x_at(d))
    net.later(small_x.at[pl.ds(0, NX - 1)], sx_pair)

    net.arrived(gkv_cr, gc_pair[1])
    gkv_xs[...] = (gkv[c].astype(F32) + gkv_cr[...].astype(F32)).astype(BF16)
    for d in far_first(NX):
        net.send(gkv_xs.at[(x + d) % NX], gkv_xr.at[d - 1], gx_pair, net.x_at(d))
    net.later(gkv_xr, gx_pair)

    outs.to_x()
    queries.to_z()
    outs.to_z()
    net.arrived(small_x.at[pl.ds(0, NX - 1)], sx_pair[1])
    line = small_x[0]
    for i in range(1, NX):
        line += small_x[i]
    small_z[z] = line
    for d in far_first(nz):
        net.send(small_z.at[z], small_z.at[z], sz_pair, net.z_at(d))
    net.later(small_z.at[pl.ds(0, nz - 1)], sz_pair)

    total = gkv_xs[x].astype(F32)
    net.arrived(gkv_xr, gx_pair[1])
    for d in range(1, NX):
        total += gkv_xr[d - 1].astype(F32)
    gkv_zs[...] = total.astype(BF16)
    for d in far_first(nz):
        target = (z + d) % nz

        @pl.when(target % 2 == c)
        def _(d=d, target=target):
            net.send(gkv_zs.at[target // 2], gkv_zr.at[d - 1], gz_pair, net.at(z=target))

    @net.ends.append
    def _():
        @pl.when(hub)
        def _():
            net.sent(gkv_zs.at[pl.ds(0, half_z - 1)], gz_pair)

        @pl.when(jnp.logical_not(hub))
        def _():
            net.sent(gkv_zs, gz_pair)

    hidden_1.back_z()
    hidden_2.back_z()
    outs.back_z()
    queries.back_z()

    hidden_1.back_x()
    hidden_2.back_x()

    net.arrived(small_z.at[pl.ds(0, nz - 1)], sz_pair[1])
    line = small_z[0]
    for i in range(1, nz):
        line += small_z[i]
    small_ref[c] = line
    net.send(small_ref.at[c], small_ref.at[c], sf_pair, net.sibling())
    net.later(small_cr, sf_pair)

    @pl.when(hub)
    def _():
        net.arrived(gkv_zr, gz_pair[1])
        total = gkv_zs[z // 2].astype(F32)
        for d in range(1, nz):
            total += gkv_zr[d - 1].astype(F32)
        gkv_sum[...] = total.reshape(gkv_sum.shape)
        net.send(gkv_sum.at[other], okv_ref, gf_pair, net.sibling())
        okv_ref[...] = gkv_sum[c]

    @net.ends.append
    def _():
        @pl.when(hub)
        def _():
            net.sent(gkv_sum.at[other], gf_pair)

    outs.back_x()
    queries.back_x()
    for chunk in sums:
        chunk.back_core()

    @pl.when(jnp.logical_not(hub))
    def _():
        net.arrived(okv_ref, gf_pair[1])

    net.arrived(small_ref.at[other], sf_pair[1])
    stores = [
        pltpu.make_async_copy(okv_ref, okv_hbm, local.at[10]),
        pltpu.make_async_copy(small_ref, small_hbm, local.at[11]),
    ]
    for store in stores:
        store.start()
    for i, chunk in enumerate(sums):
        chunk.end()
        stores.append(pltpu.make_async_copy(ws_full.at[i], ws_hbm.at[i], local.at[12 + i]))
        stores[-1].start()
    for store in stores:
        store.wait()
    net.finish()
    assert net.used <= SEMAPHORES, net.used


def write_kernel(
    ws_hbm,
    small_hbm,
    kv_hbm,
    wq_ref,
    wo_ref,
    wh_ref,
    logit_ref,
    gain_ref,
    keys_ref,
    values_ref,
    ws_ref,
    small_ref,
    kv_ref,
    sems,
):
    loads = [pltpu.make_async_copy(ws_hbm.at[i], ws_ref.at[i], sems.at[i]) for i in range(4)]
    loads.append(pltpu.make_async_copy(small_hbm, small_ref, sems.at[4]))
    loads.append(pltpu.make_async_copy(kv_hbm, kv_ref, sems.at[5]))
    for load in loads:
        load.start()

    def block(i, c, x):
        rows = []
        for r in range(3):
            rows.append(jnp.concatenate([ws_ref[i, c, x, 3 * r + l] for l in range(3)], axis=1))
        return jnp.concatenate(rows, axis=0).astype(F32)

    depth = wh_ref.shape[0] // 2
    for i in range(4):
        loads[i].wait()
        for c in range(NC):
            for x in range(NX):
                if i < 2:
                    row = i * depth + (c * NX + x) * 48
                    wh_ref[row : row + 48, :] = block(i, c, x)
                else:
                    ref = wo_ref if i == 2 else wq_ref
                    ref[x * 48 : x * 48 + 48, c * 384 : c * 384 + 384] = block(i, c, x)
    loads[4].wait()
    lines = [small_ref[i // 5, i % 5] for i in range(9)]
    for i in range(3):
        logit_ref[128 * i : 128 * (i + 1)] = lines[i].reshape(128)
    for i in range(6):
        gain_ref[128 * i : 128 * (i + 1)] = lines[3 + i].reshape(128)
    loads[5].wait()
    columns = keys_ref.shape[1]
    keys_ref[...] = kv_ref[:, :columns]
    values_ref[...] = kv_ref[:, columns:]


def solution(mesh):
    nz = mesh.shape["pts"] // (NX * NC)
    ny = mesh.shape["head"]
    half_z = nz // 2

    def on_device(pool, index, labels, w_query, keys, values, w_out, out_gain, w_hidden, w_logit):
        points, columns = index.shape[0], keys.shape[1]
        width, hidden = w_hidden.shape
        latents = keys.shape[0] * nz * NX * NC
        heads = columns // HD
        vmem = pltpu.VMEM
        tile = (16, 128)
        wide = (16, 2 * columns)
        shapes = [
            jax.ShapeDtypeStruct((4, NC, NX, PIECES) + tile, BF16),
            jax.ShapeDtypeStruct((NC, 5, 1, 128), F32),
            jax.ShapeDtypeStruct((8, 2 * columns), F32),
        ]
        scratch = [vmem(shape.shape, shape.dtype) for shape in shapes] + [
            vmem((columns, pool.shape[0]), BF16),
            vmem((points,), jnp.int32),
            vmem((points,), jnp.int32),
            vmem((width,), BF16),
            vmem((hidden,), BF16),
            vmem((columns, width), BF16),
            vmem(keys.shape, BF16),
            vmem(keys.shape, BF16),
            vmem((ny, points, 128), BF16),
            vmem((ny, points // 2, 128), BF16),
            vmem((points, width), BF16),
            vmem((ny, columns, width), BF16),
            vmem((ny, width, hidden), BF16),
            vmem((ny, 1, hidden), F32),
            vmem((8, 2 * columns), F32),
            vmem((8, 2 * columns), F32),
            vmem((2, NX, half_z) + wide, BF16),
            vmem((points, columns), BF16),
            vmem((heads, latents, points), BF16),
            vmem((columns, points), BF16),
            vmem((ny, heads, points // 2, 128), BF16),
            vmem((2 * columns, latents), BF16),
            vmem((heads, latents, points), BF16),
            vmem((points, width), F32),
            vmem((points, width), BF16),
            vmem((ny, points, hidden), BF16),
            vmem((ny, points, hidden), F32),
            vmem((ny, points, hidden), BF16),
            vmem((4, NC, NX, PIECES) + tile, BF16),
            vmem((4, NX, PIECES) + tile, BF16),
            vmem((4, NX, PIECES) + tile, BF16),
            vmem((4, NX - 1, PIECES) + tile, BF16),
            vmem((4, PIECES) + tile, BF16),
            vmem((4, nz - 1) + tile, BF16),
            vmem((2, NX, half_z) + wide, BF16),
            vmem((NX, half_z) + wide, BF16),
            vmem((NX, half_z) + wide, BF16),
            vmem((NX - 1, half_z) + wide, BF16),
            vmem((half_z,) + wide, BF16),
            vmem((nz - 1,) + wide, BF16),
            vmem((2, 8, 2 * columns), F32),
            vmem((NC, 5, 1, 128), F32),
            vmem((5, 1, 128), F32),
            vmem((NX, 5, 1, 128), F32),
            vmem((nz, 5, 1, 128), F32),
            pltpu.SemaphoreType.DMA((16,)),
            pltpu.SemaphoreType.DMA((SEMAPHORES,)),
        ]
        whole = pl.BlockSpec(memory_space=pltpu.VMEM)
        sums = pl.pallas_call(
            lambda *refs: kernel(nz, ny, *refs),
            out_shape=shapes,
            in_specs=[pl.BlockSpec(memory_space=pl.ANY)] * 10,
            out_specs=[pl.BlockSpec(memory_space=pl.ANY)] * 3,
            scratch_shapes=scratch,
            compiler_params=pltpu.CompilerParams(
                collective_id=0, has_side_effects=True, vmem_limit_bytes=56 * 1024 * 1024
            ),
        )(pool.T, index, labels, out_gain, w_logit, w_query.T, keys, values, w_out, w_hidden)
        outs = pl.pallas_call(
            write_kernel,
            out_shape=[
                jax.ShapeDtypeStruct((columns, width), F32),
                jax.ShapeDtypeStruct((columns, width), F32),
                jax.ShapeDtypeStruct((width, hidden), F32),
                jax.ShapeDtypeStruct((hidden,), F32),
                jax.ShapeDtypeStruct((width,), F32),
                jax.ShapeDtypeStruct(keys.shape, F32),
                jax.ShapeDtypeStruct(keys.shape, F32),
            ],
            in_specs=[pl.BlockSpec(memory_space=pltpu.HBM)] * 3,
            out_specs=[whole] * 7,
            scratch_shapes=[vmem(shape.shape, shape.dtype) for shape in shapes]
            + [pltpu.SemaphoreType.DMA((6,))],
            compiler_params=pltpu.CompilerParams(vmem_limit_bytes=60 * 1024 * 1024),
        )(*sums)
        return (outs[0].T,) + tuple(outs[1:])

    return jax.shard_map(
        on_device,
        mesh=mesh,
        in_specs=(
            P("pts", "head"),
            P("pts"),
            P("pts"),
            P(None, "head"),
            P("pts", "head"),
            P("pts", "head"),
            P("head", None),
            P(),
            P(None, "head"),
            P("head"),
        ),
        out_specs=(
            P(None, "head"),
            P("head", None),
            P(None, "head"),
            P("head"),
            P(),
            P("pts", "head"),
            P("pts", "head"),
        ),
        check_vma=False,
    )
```

```python
import jax
import jax.numpy as jnp
from jax import lax
from jax.experimental import pallas as pl
from jax.experimental.pallas import tpu as pltpu
from jax.sharding import PartitionSpec as P

HD = 64
EPSILON = 1e-05
NX = 4
NC = 2
SEMAPHORES = 96
MESH = pl.DeviceIdType.MESH
F32 = jnp.float32
BF16 = jnp.bfloat16


def dot(a, b):
    return jnp.dot(a, b, preferred_element_type=F32)


def dot_nt(a, b):
    return lax.dot_general(a, b, (((1,), (1,)), ((), ())), preferred_element_type=F32)


def far_first(n):
    return sorted(range(1, n), key=lambda d: -min(d, n - d))


def packed(block):
    half = block.shape[0] // 2
    return block[:, :128], jnp.concatenate([block[:half, 128:], block[half:, 128:]], axis=1)


def folded(block):
    half = block.shape[0] // 2
    return jnp.concatenate([block[:half], block[half:]], axis=1)


def unfolded(block):
    return jnp.concatenate([block[:, :64], block[:, 64:]], axis=0)


def unpacked(wide, narrow):
    return jnp.concatenate([wide, jnp.concatenate([narrow[:, :64], narrow[:, 64:]], axis=0)], axis=1)


class Links:
    def __init__(self, nz, ny, sems):
        self.nz, self.ny, self.sems, self.used = nz, ny, sems, 0
        p = lax.axis_index("pts")
        self.y = lax.axis_index("head")
        self.c = p % NC
        self.x = (p // NC) % NX
        self.z = p // (NC * NX)
        self.other = 1 - self.c
        self.ends = []

    def at(self, x=None, y=None, z=None, c=None):
        x = self.x if x is None else x
        y = self.y if y is None else y
        z = self.z if z is None else z
        c = self.c if c is None else c
        return (z * (NC * NX) + x * NC + c, y)

    def x_at(self, d):
        return self.at(x=(self.x + d) % NX)

    def y_at(self, d):
        return self.at(y=(self.y + d) % self.ny)

    def z_at(self, d):
        return self.at(z=(self.z + d) % self.nz)

    def sibling(self):
        return self.at(c=self.other)

    def take(self, count):
        first = self.used
        self.used += count
        return first

    def copy(self, src, dst, send, recv, device):
        return pltpu.make_async_remote_copy(
            src_ref=src,
            dst_ref=dst,
            send_sem=self.sems.at[send],
            recv_sem=self.sems.at[recv if isinstance(recv, int) else sum(recv)],
            device_id=device,
            device_id_type=MESH,
        )

    def pair(self):
        return self.take(1), self.take(1)

    def send(self, src, dst, pair, device):
        self.copy(src, dst, pair[0], pair[1], device).start()

    def arrived(self, total, recv):
        self.copy(total, total, 0, recv, self.sibling()).wait_recv()

    def sent(self, total, pair):
        self.copy(total, total, pair[0], 0, self.sibling()).wait_send()

    def later(self, total, pair):
        self.ends.append(lambda: self.sent(total, pair))

    def finish(self):
        for end in self.ends:
            end()


class WeightSum:
    def __init__(self, net, refs, mirrored):
        self.net, self.mirrored = net, mirrored
        self.part, self.cr, self.xs, self.xr, self.zs, self.zr, self.full = refs
        self.count = self.zs.shape[0]
        self.core, self.x, self.z = net.pair(), net.pair(), net.pair()
        self.gz, self.gx, self.gc = net.pair(), net.pair(), net.pair()
        self.piece, self.reduces = self.role(net.z)

    def role(self, z):
        nz = self.net.nz
        spot = (nz - 1 - z) if self.mirrored else z
        piece = (self.count * spot + nz - 1) // nz
        return jnp.minimum(piece, self.count - 1), (nz * piece) // self.count == spot

    def put(self, c, x, block, slot=0):
        block = block.astype(BF16)
        for j in range(9):
            r, l = 16 * (j // 3), 128 * (j % 3)
            self.part[c, x, j, 16 * slot : 16 * slot + 16] = block[r : r + 16, l : l + 128]

    def start(self):
        net = self.net
        net.send(self.part.at[net.other], self.cr, self.core, net.sibling())
        net.later(self.cr, self.core)

    def to_x(self):
        net = self.net
        net.arrived(self.cr, self.core[1])
        self.xs[...] = (self.part[net.c].astype(F32) + self.cr[...].astype(F32)).astype(BF16)
        for d in far_first(NX):
            target = (net.x + d) % NX
            net.send(self.xs.at[target], self.xr.at[d - 1], self.x, net.x_at(d))
        net.later(self.xr, self.x)

    def to_z(self):
        net = self.net
        net.arrived(self.xr, self.x[1])
        total = self.xs[net.x].astype(F32)
        for d in range(1, NX):
            total += self.xr[d - 1].astype(F32)
        self.zs[...] = total.astype(BF16)
        for d in far_first(net.nz):
            spot = (net.z + d) % net.nz
            piece, reduces = self.role(spot)

            @pl.when(reduces)
            def _(d=d, piece=piece, spot=spot):
                net.send(self.zs.at[piece], self.zr.at[d - 1], self.z, net.at(z=spot))

        @net.ends.append
        def _():
            self.pieces(lambda total: net.sent(total, self.z))

    def pieces(self, wait):
        @pl.when(self.reduces)
        def _():
            wait(self.zs.at[pl.ds(0, self.count - 1)])

        @pl.when(jnp.logical_not(self.reduces))
        def _():
            wait(self.zs)

    def back_z(self):
        net = self.net
        tile = self.full.at[net.c, net.x, self.piece]

        @pl.when(self.reduces)
        def _():
            net.arrived(self.zr, self.z[1])
            total = self.zs[self.piece].astype(F32)
            for d in range(1, net.nz):
                total += self.zr[d - 1].astype(F32)
            self.full[net.c, net.x, self.piece] = total.astype(BF16)
            for d in far_first(net.nz):
                net.send(tile, tile, self.gz, net.z_at(d))

        @net.ends.append
        def _():
            @pl.when(self.reduces)
            def _():
                net.sent(self.zr, self.gz)

    def back_x(self):
        net = self.net
        self.pieces(lambda total: net.arrived(total, self.gz[1]))
        mine = self.full.at[net.c, net.x]
        for d in far_first(NX):
            net.send(mine, mine, self.gx, net.x_at(d))
        net.later(self.xr, self.gx)

    def back_core(self):
        net = self.net
        net.arrived(self.xr, self.gx[1])
        mine = self.full.at[net.c]
        net.send(mine, mine, self.gc, net.sibling())
        net.later(mine, self.gc)

    def end(self):
        net = self.net
        net.arrived(self.full.at[net.other], self.gc[1])


def kernel(
    nz,
    ny,
    pool_hbm,
    index_hbm,
    label_hbm,
    gain_hbm,
    w_logit_hbm,
    w_query_hbm,
    keys_hbm,
    values_hbm,
    w_out_hbm,
    w_hidden_hbm,
    hid_hbm,
    out_hbm,
    que_hbm,
    okv_hbm,
    hid_full,
    out_full,
    que_full,
    okv_ref,
    pool,
    index,
    label_ref,
    gain_ref,
    w_logit,
    w_query,
    keys,
    values,
    rows_wide,
    rows_narrow,
    rows_in,
    wo_full,
    wh_full,
    wl_full,
    kv_own,
    kvx,
    kv_buf,
    q_ref,
    probs,
    att_t,
    att_buf,
    kv_t_ref,
    ds_ref,
    normal_ref,
    normed_ref,
    act_ref,
    slope_ref,
    dh_ref,
    hid_part,
    hid_cr,
    hid_xs,
    hid_xr,
    hid_zs,
    hid_zr,
    out_part,
    out_cr,
    out_xs,
    out_xr,
    out_zs,
    out_zr,
    que_part,
    que_cr,
    que_xs,
    que_xr,
    que_zs,
    que_zr,
    gkv,
    gkv_cr,
    gkv_xs,
    gkv_xr,
    gkv_zs,
    gkv_zr,
    gkv_sum,
    local,
    sems,
):
    net = Links(nz, ny, sems)
    x, y, z, c, other = net.x, net.y, net.z, net.c, net.other
    points, width = rows_in.shape
    half_z = nz // 2
    hidden = wh_full.shape[2]

    barrier = pltpu.get_barrier_semaphore()
    partners = [net.sibling()]
    partners += [net.x_at(d) for d in range(1, NX)]
    partners += [net.y_at(d) for d in range(1, ny)]
    partners += [net.z_at(d) for d in far_first(nz)]
    for device in partners:
        pl.semaphore_signal(barrier, inc=1, device_id=device, device_id_type=MESH)

    loads = [
        pltpu.make_async_copy(source, target, local.at[i])
        for i, (source, target) in enumerate(
            (
                (keys_hbm, keys),
                (values_hbm, values),
                (index_hbm, index),
                (pool_hbm, pool),
                (w_out_hbm, wo_full.at[y]),
                (w_hidden_hbm, wh_full.at[y]),
                (w_query_hbm, w_query),
                (label_hbm, label_ref),
                (gain_hbm, gain_ref),
                (w_logit_hbm, w_logit),
            )
        )
    ]
    for load in loads:
        load.start()
    loads[0].wait()
    loads[1].wait()
    kv_own[...] = jnp.concatenate([keys[...].astype(F32), values[...].astype(F32)], axis=1)
    pl.semaphore_wait(barrier, len(partners))

    hub = z % 2 == c
    kvx_pair, kx_pair, kc_pair = net.pair(), net.pair(), net.pair()
    s_kz, r_kz = net.take(1), net.take(half_z)
    kv_tile = kv_buf.at[c, x, z // 2]

    @pl.when(jnp.logical_not(hub))
    def _():
        net.send(kv_own, kvx, kvx_pair, net.sibling())

    loads[2].wait()
    loads[3].wait()
    spots = lax.broadcasted_iota(jnp.int32, (pool.shape[1], points), 0)
    chosen = jnp.where(spots == index[...].reshape(1, points), 1.0, 0.0).astype(BF16)
    picked = dot(pool[...], chosen).T.astype(BF16)
    wide, narrow = packed(picked)
    rows_wide[y] = wide
    rows_narrow[y] = narrow

    wide_pair, narrow_pair = net.pair(), net.pair()
    for d in far_first(ny):
        net.send(rows_wide.at[y], rows_wide.at[y], wide_pair, net.y_at(d))
        net.send(rows_narrow.at[y], rows_narrow.at[y], narrow_pair, net.y_at(d))
    others = pl.ds(0, ny - 1)
    net.later(rows_wide.at[others], wide_pair)
    net.later(rows_narrow.at[others], narrow_pair)

    @pl.when(hub)
    def _():
        net.arrived(kvx, kvx_pair[1])
        own, extra = kv_own[...], kvx[...]
        low = jnp.where(c == 0, own, extra)
        high = jnp.where(c == 0, extra, own)
        kv_buf[c, x, z // 2] = jnp.concatenate([low, high], axis=0).astype(BF16)
        for d in far_first(nz):
            net.send(kv_tile, kv_tile, (s_kz, (r_kz, z // 2)), net.z_at(d))

    @net.ends.append
    def _():
        @pl.when(hub)
        def _():
            net.sent(gkv_zr, (s_kz, 0))

        @pl.when(jnp.logical_not(hub))
        def _():
            net.sent(kv_own, kvx_pair)

    wo_pair, near_pair, far_pair, wl_pair = net.pair(), net.pair(), net.pair(), net.pair()
    wx_pair, fo_pair, fn_pair, ff_pair = net.pair(), net.pair(), net.pair(), net.pair()
    o_rows, h_rows = wo_full.shape[1] // 2, wh_full.shape[1] // 2
    x_rows = h_rows // NX
    far = ny // 2

    def wo_half(owner, core):
        return wo_full.at[owner, pl.ds(core * o_rows, o_rows)]

    def wh_half(owner, core):
        return wh_full.at[owner, pl.ds(core * h_rows, h_rows)]

    def wh_part(owner, core, part):
        return wh_full.at[owner, pl.ds(core * h_rows + part * x_rows, x_rows)]

    def wo_bytes(count):
        return wo_full.at[pl.ds(0, count), pl.ds(0, o_rows)]

    def wh_bytes(count):
        return wh_full.at[pl.ds(0, count), pl.ds(0, h_rows)]

    loads[4].wait()
    for d in far_first(ny):
        net.send(wo_half(y, c), wo_half(y, c), wo_pair, net.y_at(d))
    net.later(wo_bytes(ny - 1), wo_pair)
    loads[5].wait()
    loads[9].wait()
    wl_full[y] = w_logit[...].astype(F32).reshape(1, hidden)
    for d in far_first(ny):
        if d == far:
            net.send(wh_part(y, c, x), wh_part(y, c, x), far_pair, net.y_at(d))
        else:
            net.send(wh_half(y, c), wh_half(y, c), near_pair, net.y_at(d))
        net.send(wl_full.at[y], wl_full.at[y], wl_pair, net.y_at(d))
    net.later(wh_part(0, 0, 0), far_pair)
    net.later(wh_bytes(ny - 2), near_pair)
    net.later(wl_full.at[others], wl_pair)

    side = jnp.where(jnp.logical_and(z % 2 == 0, c == 1), half_z - 1, 1)
    blocks = []
    for k in range(half_z):
        away = (k + 1) // 2
        step = away * side if k % 2 else (half_z - away) * side
        block = (z // 2 + step) % half_z
        blocks.append(block)
        tile = kv_buf.at[c, x, block]
        if k:
            net.arrived(tile, (r_kz, block))
        else:

            @pl.when(jnp.logical_not(hub))
            def _(tile=tile, block=block):
                net.arrived(tile, (r_kz, block))

        for d in far_first(NX):
            net.send(tile, tile, kx_pair, net.x_at(d))
    net.later(gkv_xr, kx_pair)
    net.arrived(rows_wide.at[others], wide_pair[1])
    net.arrived(rows_narrow.at[others], narrow_pair[1])
    rows_in[...] = jnp.concatenate(
        [unpacked(rows_wide[i], rows_narrow[i]) for i in range(ny)], axis=1
    )
    loads[6].wait()
    query = dot_nt(rows_in[...], w_query[...]).astype(BF16)
    q_ref[...] = query
    own = kv_buf.at[c, x]
    net.send(own, own, kc_pair, net.sibling())
    net.arrived(gkv_xr, kx_pair[1])
    for d in range(1, NX):
        block = kv_buf.at[c, (x + NX - d) % NX]
        net.send(block, block, kc_pair, net.sibling())
    net.later(gkv_xs, kc_pair)
    far_y = (y + ny - far) % ny
    net.arrived(wo_bytes(ny - 1), wo_pair[1])
    for d in range(1, ny):
        block = wo_half((y + ny - d) % ny, c)
        net.send(block, block, fo_pair, net.sibling())
    net.later(wo_bytes(ny - 1), fo_pair)
    net.arrived(wh_part(0, 0, 0), far_pair[1])
    for d in far_first(NX):
        net.send(wh_part(far_y, c, x), wh_part(far_y, c, x), wx_pair, net.x_at(d))
    three = wh_full.at[0, pl.ds(0, (NX - 1) * x_rows)]
    net.later(three, wx_pair)
    net.arrived(gkv_xs, kc_pair[1])

    columns = w_query.shape[0]
    heads = columns // HD
    latents = 16 * half_z * NX * 2
    kv = kv_buf[...].reshape(latents, 2 * columns)
    kv_t_ref[...] = kv.T
    k_all, v_all = kv[:, :columns], kv[:, columns:]
    att_pair = net.pair()
    lane_head = lax.broadcasted_iota(jnp.int32, (points, columns), 1) // HD
    scale = HD ** (-0.5)
    log2e = 1.4426950408889634
    for h in range(heads):
        q_h = jnp.where(lane_head == h, query, jnp.zeros_like(query))
        raw = dot_nt(k_all, q_h)
        top = jnp.max(raw, axis=0, keepdims=True)
        e = jnp.exp2((raw - top) * (scale * log2e))
        p_h = (e * (1.0 / jnp.sum(e, axis=0, keepdims=True))).astype(BF16)
        probs[h] = p_h
        v_t = kv_t_ref[columns + h * HD : columns + (h + 1) * HD]
        att_h = dot(v_t, p_h).astype(BF16)
        att_t[h * HD : (h + 1) * HD] = att_h
        att_buf[y, h] = folded(att_h.T)
        for d in far_first(ny):
            net.send(att_buf.at[y, h], att_buf.at[y, h], att_pair, net.y_at(d))

    net.later(att_buf.at[others], att_pair)
    net.arrived(wl_full.at[others], wl_pair[1])
    net.arrived(wh_bytes(ny - 2), near_pair[1])
    for d in range(1, ny):
        if d != far:
            block = wh_half((y + ny - d) % ny, c)
            net.send(block, block, fn_pair, net.sibling())
    net.later(wh_bytes(ny - 2), fn_pair)
    net.arrived(three, wx_pair[1])
    net.send(wh_half(far_y, c), wh_half(far_y, c), ff_pair, net.sibling())
    net.later(wh_half(0, 0), ff_pair)
    net.arrived(wo_bytes(ny - 1), fo_pair[1])
    net.arrived(att_buf.at[others], att_pair[1])

    attended = jnp.concatenate(
        [unfolded(att_buf[i, h]) for i in range(ny) for h in range(heads)], axis=1
    )
    mixed = rows_in[...].astype(F32) + dot(attended, wo_full[...].reshape(width, width))
    center = mixed - jnp.mean(mixed, axis=1, keepdims=True)
    rstd = lax.rsqrt(jnp.mean(center * center, axis=1, keepdims=True) + EPSILON)
    loads[8].wait()
    gain = gain_ref[...].astype(F32).reshape(1, width)
    normal = center * rstd
    normal_ref[...] = normal
    normed_ref[...] = (normal * gain).astype(BF16)

    net.arrived(wh_bytes(ny - 2), fn_pair[1])
    net.arrived(wh_half(0, 0), ff_pair[1])

    root = 0.7978845608028654
    cubic = 0.044715
    logit = jnp.zeros((points, 1), F32)
    for i in range(ny):
        v = dot(normed_ref[...], wh_full[i])
        v2 = v * v
        gate = 0.5 + 0.5 * jnp.tanh(v * (root + (root * cubic) * v2))
        smooth = v * gate
        act = smooth.astype(BF16)
        act_ref[i] = act
        slope_ref[i] = gate + smooth * (1.0 - gate) * (2.0 * root + (6.0 * root * cubic) * v2)
        logit += jnp.sum(act.astype(F32) * wl_full[i], axis=1, keepdims=True)
    total_points = points * nz * NX * NC
    loads[7].wait()
    label = label_ref[...].astype(F32).reshape(1, points)
    label = jnp.broadcast_to(label, (8, points)).T[:, 0:1]
    d_logit = (jax.nn.sigmoid(logit) - label) * total_points ** (-0.5)
    for i in range(ny):
        dh_ref[i] = (d_logit * wl_full[i] * slope_ref[i]).astype(BF16)

    hidden_sum = WeightSum(net, (hid_part, hid_cr, hid_xs, hid_xr, hid_zs, hid_zr, hid_full), False)
    out_sum = WeightSum(net, (out_part, out_cr, out_xs, out_xr, out_zs, out_zr, out_full), True)
    query_sum = WeightSum(net, (que_part, que_cr, que_xs, que_xr, que_zs, que_zr, que_full), False)
    sums = (hidden_sum, out_sum, query_sum)

    normed_t = normed_ref[...].T
    depth = normed_t.shape[0] // 2
    for k in range(2):
        grad = dot(normed_t[k * depth : (k + 1) * depth], dh_ref[y])
        for cc in range(NC):
            for xx in range(NX):
                row = (cc * NX + xx) * 48
                hidden_sum.put(cc, xx, grad[row : row + 48], k)
    hidden_sum.start()
    grad_logit = jnp.sum(d_logit * act_ref[y].astype(F32), axis=0, keepdims=True)

    d_normed = dot_nt(dh_ref[0], wh_full[0])
    for i in range(1, ny):
        d_normed += dot_nt(dh_ref[i], wh_full[i])
    normal = normal_ref[...]
    both = d_normed * normal
    grad_gain = jnp.sum(both, axis=0, keepdims=True)
    scaled = d_normed * gain
    d_mixed = rstd * (
        scaled
        - jnp.mean(scaled, axis=1, keepdims=True)
        - normal * jnp.mean(both * gain, axis=1, keepdims=True)
    )
    d_mixed = d_mixed.astype(BF16)

    hidden_sum.to_x()

    lines = [grad_logit[:, 128 * i : 128 * (i + 1)] for i in range(3)]
    lines += [grad_gain[:, 128 * i : 128 * (i + 1)] for i in range(6)]
    for i in range(NC * NX):
        second = lines[8] if i == 0 else jnp.zeros((1, 128), F32)
        block = jnp.concatenate([lines[i], second, jnp.zeros((14, 128), F32)], axis=0)
        que_part[i // NX, i % NX, 9] = block.astype(BF16)

    def block_rows(chunk, grad):
        for cc in range(NC):
            for xx in range(NX):
                chunk.put(cc, xx, grad[xx * 48 : xx * 48 + 48, cc * 384 : cc * 384 + 384])

    block_rows(out_sum, dot(att_t[...], d_mixed))
    out_sum.start()
    w_out = wo_full[y]
    d_att = dot_nt(d_mixed, w_out).astype(BF16)
    d_att_t = dot_nt(w_out, d_mixed).astype(BF16)

    query = q_ref[...]
    v_all = kv_buf[...].reshape(latents, 2 * columns)[:, columns:]
    d_query = []
    for h in range(heads):
        rows = slice(h * HD, (h + 1) * HD)
        d_att_h = jnp.where(lane_head == h, d_att, jnp.zeros_like(d_att))
        delta = jnp.sum(d_att_t[rows].astype(F32) * att_t[rows].astype(F32), axis=0, keepdims=True)
        d_probs = dot_nt(v_all, d_att_h)
        d_scores = (probs[h].astype(F32) * (d_probs - delta) * scale).astype(BF16)
        ds_ref[h] = d_scores
        d_query.append(dot(kv_t_ref[rows], d_scores).astype(BF16))
        if h == 0:
            out_sum.to_x()
    block_rows(query_sum, dot(jnp.concatenate(d_query, axis=0), rows_in[...]))
    query_sum.start()
    hidden_sum.to_z()

    grad_k = jnp.zeros((latents, columns), F32)
    grad_v = jnp.zeros((latents, columns), F32)
    for h in range(heads):
        d_att_h = jnp.where(lane_head == h, d_att, jnp.zeros_like(d_att))
        q_h = jnp.where(lane_head == h, query, jnp.zeros_like(query))
        grad_k += dot(ds_ref[h], q_h)
        grad_v += dot(probs[h], d_att_h)
        if h == 0:
            query_sum.to_x()
            out_sum.to_z()
    grads = jnp.concatenate([grad_k, grad_v], axis=1).astype(BF16)
    gkv[...] = grads.reshape(gkv.shape)
    gc_pair, gx_pair, gz_pair, gf_pair = net.pair(), net.pair(), net.pair(), net.pair()
    net.send(gkv.at[other], gkv_cr, gc_pair, net.sibling())
    net.later(gkv_cr, gc_pair)

    net.arrived(gkv_cr, gc_pair[1])
    gkv_xs[...] = (gkv[c].astype(F32) + gkv_cr[...].astype(F32)).astype(BF16)
    for d in far_first(NX):
        net.send(gkv_xs.at[(x + d) % NX], gkv_xr.at[d - 1], gx_pair, net.x_at(d))
    net.later(gkv_xr, gx_pair)

    query_sum.to_z()
    hidden_sum.back_z()
    out_sum.back_z()
    query_sum.back_z()

    total = gkv_xs[x].astype(F32)
    net.arrived(gkv_xr, gx_pair[1])
    for d in range(1, NX):
        total += gkv_xr[d - 1].astype(F32)
    gkv_zs[...] = total.astype(BF16)
    for d in far_first(nz):
        target = (z + d) % nz

        @pl.when(target % 2 == c)
        def _(d=d, target=target):
            net.send(gkv_zs.at[target // 2], gkv_zr.at[d - 1], gz_pair, net.at(z=target))

    @net.ends.append
    def _():
        @pl.when(hub)
        def _():
            net.sent(gkv_zs.at[pl.ds(0, half_z - 1)], gz_pair)

        @pl.when(jnp.logical_not(hub))
        def _():
            net.sent(gkv_zs, gz_pair)

    hidden_sum.back_x()
    out_sum.back_x()
    query_sum.back_x()

    @pl.when(hub)
    def _():
        net.arrived(gkv_zr, gz_pair[1])
        total = gkv_zs[z // 2].astype(F32)
        for d in range(1, nz):
            total += gkv_zr[d - 1].astype(F32)
        gkv_sum[...] = total.reshape(gkv_sum.shape)
        net.send(gkv_sum.at[other], okv_ref, gf_pair, net.sibling())
        okv_ref[...] = gkv_sum[c]

    @net.ends.append
    def _():
        @pl.when(hub)
        def _():
            net.sent(gkv_sum.at[other], gf_pair)

    for chunk in sums:
        chunk.back_core()

    @pl.when(jnp.logical_not(hub))
    def _():
        net.arrived(okv_ref, gf_pair[1])

    stores = [pltpu.make_async_copy(okv_ref, okv_hbm, local.at[10])]
    stores[0].start()
    places = ((hid_full, hid_hbm), (out_full, out_hbm), (que_full, que_hbm))
    for i, (chunk, (held, target)) in enumerate(zip(sums, places)):
        chunk.end()
        stores.append(pltpu.make_async_copy(held, target, local.at[11 + i]))
        stores[-1].start()
    for store in stores:
        store.wait()
    net.finish()
    assert net.used <= SEMAPHORES, net.used


def write_kernel(
    hid_hbm,
    out_hbm,
    que_hbm,
    kv_hbm,
    wq_ref,
    wo_ref,
    wh_ref,
    logit_ref,
    gain_ref,
    keys_ref,
    values_ref,
    hid_ref,
    out_ref,
    que_ref,
    kv_ref,
    sems,
):
    pairs = ((hid_hbm, hid_ref), (out_hbm, out_ref), (que_hbm, que_ref), (kv_hbm, kv_ref))
    loads = [pltpu.make_async_copy(a, b, sems.at[i]) for i, (a, b) in enumerate(pairs)]
    for load in loads:
        load.start()

    def block(ref, c, x, slot=0):
        rows = []
        for r in range(3):
            tiles = [ref[c, x, 3 * r + l, 16 * slot : 16 * slot + 16] for l in range(3)]
            rows.append(jnp.concatenate(tiles, axis=1))
        return jnp.concatenate(rows, axis=0).astype(F32)

    depth = wh_ref.shape[0] // 2
    parts = [(c, x) for c in range(NC) for x in range(NX)]
    loads[0].wait()
    for slot in range(2):
        for c, x in parts:
            row = slot * depth + (c * NX + x) * 48
            wh_ref[row : row + 48, :] = block(hid_ref, c, x, slot)
    for load, source, target in ((loads[1], out_ref, wo_ref), (loads[2], que_ref, wq_ref)):
        load.wait()
        for c, x in parts:
            target[x * 48 : x * 48 + 48, c * 384 : c * 384 + 384] = block(source, c, x)
    vectors = [que_ref[c, x, 9].astype(F32) for c, x in parts]
    lines = [vector[0:1] for vector in vectors] + [vectors[0][1:2]]
    for i in range(3):
        logit_ref[128 * i : 128 * (i + 1)] = lines[i].reshape(128)
    for i in range(6):
        gain_ref[128 * i : 128 * (i + 1)] = lines[3 + i].reshape(128)
    loads[3].wait()
    columns = keys_ref.shape[1]
    keys_ref[...] = kv_ref[:, :columns]
    values_ref[...] = kv_ref[:, columns:]


def solution(mesh):
    nz = mesh.shape["pts"] // (NX * NC)
    ny = mesh.shape["head"]
    half_z = nz // 2

    def on_device(pool, index, labels, w_query, keys, values, w_out, out_gain, w_hidden, w_logit):
        points, columns = index.shape[0], keys.shape[1]
        width, hidden = w_hidden.shape
        latents = keys.shape[0] * nz * NX * NC
        heads = columns // HD
        vmem = pltpu.VMEM
        wide = (16, 2 * columns)
        forms = ((9, (32, 128)), (9, (16, 128)), (10, (16, 128)))
        shapes = [
            jax.ShapeDtypeStruct((NC, NX, count) + tile, BF16) for count, tile in forms
        ] + [jax.ShapeDtypeStruct((8, 2 * columns), F32)]
        buffers = []
        for count, tile in forms:
            buffers += [
                vmem((NC, NX, count) + tile, BF16),
                vmem((NX, count) + tile, BF16),
                vmem((NX, count) + tile, BF16),
                vmem((NX - 1, count) + tile, BF16),
                vmem((count,) + tile, BF16),
                vmem((nz - 1,) + tile, BF16),
            ]
        scratch = [vmem(shape.shape, shape.dtype) for shape in shapes] + [
            vmem((columns, pool.shape[0]), BF16),
            vmem((points,), jnp.int32),
            vmem((points,), jnp.int32),
            vmem((width,), BF16),
            vmem((hidden,), BF16),
            vmem((columns, width), BF16),
            vmem(keys.shape, BF16),
            vmem(keys.shape, BF16),
            vmem((ny, points, 128), BF16),
            vmem((ny, points // 2, 128), BF16),
            vmem((points, width), BF16),
            vmem((ny, columns, width), BF16),
            vmem((ny, width, hidden), BF16),
            vmem((ny, 1, hidden), F32),
            vmem((8, 2 * columns), F32),
            vmem((8, 2 * columns), F32),
            vmem((2, NX, half_z) + wide, BF16),
            vmem((points, columns), BF16),
            vmem((heads, latents, points), BF16),
            vmem((columns, points), BF16),
            vmem((ny, heads, points // 2, 128), BF16),
            vmem((2 * columns, latents), BF16),
            vmem((heads, latents, points), BF16),
            vmem((points, width), F32),
            vmem((points, width), BF16),
            vmem((ny, points, hidden), BF16),
            vmem((ny, points, hidden), F32),
            vmem((ny, points, hidden), BF16),
            *buffers,
            vmem((2, NX, half_z) + wide, BF16),
            vmem((NX, half_z) + wide, BF16),
            vmem((NX, half_z) + wide, BF16),
            vmem((NX - 1, half_z) + wide, BF16),
            vmem((half_z,) + wide, BF16),
            vmem((nz - 1,) + wide, BF16),
            vmem((2, 8, 2 * columns), F32),
            pltpu.SemaphoreType.DMA((16,)),
            pltpu.SemaphoreType.DMA((SEMAPHORES,)),
        ]
        whole = pl.BlockSpec(memory_space=pltpu.VMEM)
        sums = pl.pallas_call(
            lambda *refs: kernel(nz, ny, *refs),
            out_shape=shapes,
            in_specs=[pl.BlockSpec(memory_space=pl.ANY)] * 10,
            out_specs=[pl.BlockSpec(memory_space=pl.ANY)] * 4,
            scratch_shapes=scratch,
            compiler_params=pltpu.CompilerParams(
                collective_id=0, has_side_effects=True, vmem_limit_bytes=56 * 1024 * 1024
            ),
        )(pool.T, index, labels, out_gain, w_logit, w_query.T, keys, values, w_out, w_hidden)
        outs = pl.pallas_call(
            write_kernel,
            out_shape=[
                jax.ShapeDtypeStruct((columns, width), F32),
                jax.ShapeDtypeStruct((columns, width), F32),
                jax.ShapeDtypeStruct((width, hidden), F32),
                jax.ShapeDtypeStruct((hidden,), F32),
                jax.ShapeDtypeStruct((width,), F32),
                jax.ShapeDtypeStruct(keys.shape, F32),
                jax.ShapeDtypeStruct(keys.shape, F32),
            ],
            in_specs=[pl.BlockSpec(memory_space=pltpu.HBM)] * 4,
            out_specs=[whole] * 7,
            scratch_shapes=[vmem(shape.shape, shape.dtype) for shape in shapes]
            + [pltpu.SemaphoreType.DMA((4,))],
            compiler_params=pltpu.CompilerParams(vmem_limit_bytes=60 * 1024 * 1024),
        )(*sums)
        return (outs[0].T,) + tuple(outs[1:])

    return jax.shard_map(
        on_device,
        mesh=mesh,
        in_specs=(
            P("pts", "head"),
            P("pts"),
            P("pts"),
            P(None, "head"),
            P("pts", "head"),
            P("pts", "head"),
            P("head", None),
            P(),
            P(None, "head"),
            P("head"),
        ),
        out_specs=(
            P(None, "head"),
            P("head", None),
            P(None, "head"),
            P("head"),
            P(),
            P("pts", "head"),
            P("pts", "head"),
        ),
        check_vma=False,
    )
```

```python
import jax
import jax.numpy as jnp
from jax import lax
from jax.experimental import pallas as pl
from jax.experimental.pallas import tpu as pltpu
from jax.sharding import PartitionSpec as P

HD = 64
EPSILON = 1e-05
NX = 4
NC = 2
SEMAPHORES = 96
MESH = pl.DeviceIdType.MESH
F32 = jnp.float32
BF16 = jnp.bfloat16


def dot(a, b):
    return jnp.dot(a, b, preferred_element_type=F32)


def dot_nt(a, b):
    return lax.dot_general(a, b, (((1,), (1,)), ((), ())), preferred_element_type=F32)


def far_first(n):
    return sorted(range(1, n), key=lambda d: -min(d, n - d))


def packed(block):
    half = block.shape[0] // 2
    return block[:, :128], jnp.concatenate([block[:half, 128:], block[half:, 128:]], axis=1)


def folded(block):
    half = block.shape[0] // 2
    return jnp.concatenate([block[:half], block[half:]], axis=1)


def unfolded(block):
    return jnp.concatenate([block[:, :64], block[:, 64:]], axis=0)


def unpacked(wide, narrow):
    return jnp.concatenate([wide, jnp.concatenate([narrow[:, :64], narrow[:, 64:]], axis=0)], axis=1)


class Links:
    def __init__(self, nz, ny, sems):
        self.nz, self.ny, self.sems, self.used = nz, ny, sems, 0
        p = lax.axis_index("pts")
        self.y = lax.axis_index("head")
        self.c = p % NC
        self.x = (p // NC) % NX
        self.z = p // (NC * NX)
        self.other = 1 - self.c
        self.ends = []

    def at(self, x=None, y=None, z=None, c=None):
        x = self.x if x is None else x
        y = self.y if y is None else y
        z = self.z if z is None else z
        c = self.c if c is None else c
        return (z * (NC * NX) + x * NC + c, y)

    def x_at(self, d):
        return self.at(x=(self.x + d) % NX)

    def y_at(self, d):
        return self.at(y=(self.y + d) % self.ny)

    def z_at(self, d):
        return self.at(z=(self.z + d) % self.nz)

    def sibling(self):
        return self.at(c=self.other)

    def take(self, count):
        first = self.used
        self.used += count
        return first

    def copy(self, src, dst, send, recv, device):
        return pltpu.make_async_remote_copy(
            src_ref=src,
            dst_ref=dst,
            send_sem=self.sems.at[send],
            recv_sem=self.sems.at[recv if isinstance(recv, int) else sum(recv)],
            device_id=device,
            device_id_type=MESH,
        )

    def pair(self):
        return self.take(1), self.take(1)

    def send(self, src, dst, pair, device):
        self.copy(src, dst, pair[0], pair[1], device).start()

    def arrived(self, total, recv):
        self.copy(total, total, 0, recv, self.sibling()).wait_recv()

    def sent(self, total, pair):
        self.copy(total, total, pair[0], 0, self.sibling()).wait_send()

    def later(self, total, pair):
        self.ends.append(lambda: self.sent(total, pair))

    def finish(self):
        for end in self.ends:
            end()


class WeightSum:
    def __init__(self, net, refs, mirrored):
        self.net, self.mirrored = net, mirrored
        self.part, self.cr, self.xs, self.xr, self.zs, self.zr, self.full = refs
        self.count = self.zs.shape[0]
        self.core, self.x, self.z = net.pair(), net.pair(), net.pair()
        self.gz, self.gx, self.gc = net.pair(), net.pair(), net.pair()
        self.piece, self.reduces = self.role(net.z)

    def role(self, z):
        nz = self.net.nz
        spot = (nz - 1 - z) if self.mirrored else z
        piece = (self.count * spot + nz - 1) // nz
        return jnp.minimum(piece, self.count - 1), (nz * piece) // self.count == spot

    def put(self, c, x, block, slot=0):
        block = block.astype(BF16)
        for j in range(9):
            r, l = 16 * (j // 3), 128 * (j % 3)
            self.part[c, x, j, 16 * slot : 16 * slot + 16] = block[r : r + 16, l : l + 128]

    def start(self):
        net = self.net
        net.send(self.part.at[net.other], self.cr, self.core, net.sibling())
        net.later(self.cr, self.core)

    def to_x(self):
        net = self.net
        net.arrived(self.cr, self.core[1])
        self.xs[...] = (self.part[net.c].astype(F32) + self.cr[...].astype(F32)).astype(BF16)
        for d in far_first(NX):
            target = (net.x + d) % NX
            net.send(self.xs.at[target], self.xr.at[d - 1], self.x, net.x_at(d))
        net.later(self.xr, self.x)

    def to_z(self):
        net = self.net
        net.arrived(self.xr, self.x[1])
        total = self.xs[net.x].astype(F32)
        for d in range(1, NX):
            total += self.xr[d - 1].astype(F32)
        self.zs[...] = total.astype(BF16)
        for d in far_first(net.nz):
            spot = (net.z + d) % net.nz
            piece, reduces = self.role(spot)

            @pl.when(reduces)
            def _(d=d, piece=piece, spot=spot):
                net.send(self.zs.at[piece], self.zr.at[d - 1], self.z, net.at(z=spot))

        @net.ends.append
        def _():
            self.pieces(lambda total: net.sent(total, self.z))

    def pieces(self, wait):
        @pl.when(self.reduces)
        def _():
            wait(self.zs.at[pl.ds(0, self.count - 1)])

        @pl.when(jnp.logical_not(self.reduces))
        def _():
            wait(self.zs)

    def back_z(self):
        net = self.net
        tile = self.full.at[net.c, net.x, self.piece]

        @pl.when(self.reduces)
        def _():
            net.arrived(self.zr, self.z[1])
            total = self.zs[self.piece].astype(F32)
            for d in range(1, net.nz):
                total += self.zr[d - 1].astype(F32)
            self.full[net.c, net.x, self.piece] = total.astype(BF16)
            for d in far_first(net.nz):
                net.send(tile, tile, self.gz, net.z_at(d))

        @net.ends.append
        def _():
            @pl.when(self.reduces)
            def _():
                net.sent(self.zr, self.gz)

    def back_x(self):
        net = self.net
        self.pieces(lambda total: net.arrived(total, self.gz[1]))
        mine = self.full.at[net.c, net.x]
        for d in far_first(NX):
            net.send(mine, mine, self.gx, net.x_at(d))
        net.later(self.xr, self.gx)

    def back_core(self):
        net = self.net
        net.arrived(self.xr, self.gx[1])
        mine = self.full.at[net.c]
        net.send(mine, mine, self.gc, net.sibling())
        net.later(mine, self.gc)

    def end(self):
        net = self.net
        net.arrived(self.full.at[net.other], self.gc[1])


def kernel(
    nz,
    ny,
    pool_hbm,
    index_hbm,
    label_hbm,
    gain_hbm,
    w_logit_hbm,
    w_query_hbm,
    keys_hbm,
    values_hbm,
    w_out_hbm,
    w_hidden_hbm,
    hid_hbm,
    out_hbm,
    que_hbm,
    okv_hbm,
    hid_full,
    out_full,
    que_full,
    okv_ref,
    pool,
    index,
    label_ref,
    gain_ref,
    w_logit,
    w_query,
    keys,
    values,
    rows_wide,
    rows_narrow,
    rows_in,
    wo_full,
    wh_full,
    wl_full,
    kv_own,
    kvx,
    kv_buf,
    q_ref,
    probs,
    att_t,
    att_buf,
    kv_t_ref,
    ds_ref,
    normal_ref,
    normed_ref,
    act_ref,
    slope_ref,
    dh_ref,
    hid_part,
    hid_cr,
    hid_xs,
    hid_xr,
    hid_zs,
    hid_zr,
    out_part,
    out_cr,
    out_xs,
    out_xr,
    out_zs,
    out_zr,
    que_part,
    que_cr,
    que_xs,
    que_xr,
    que_zs,
    que_zr,
    gkv,
    gkv_cr,
    gkv_xs,
    gkv_xr,
    gkv_zs,
    gkv_zr,
    gkv_sum,
    local,
    sems,
):
    net = Links(nz, ny, sems)
    x, y, z, c, other = net.x, net.y, net.z, net.c, net.other
    points, width = rows_in.shape
    half_z = nz // 2
    hidden = wh_full.shape[2]

    barrier = pltpu.get_barrier_semaphore()
    partners = [net.sibling()]
    partners += [net.x_at(d) for d in range(1, NX)]
    partners += [net.y_at(d) for d in range(1, ny)]
    partners += [net.z_at(d) for d in far_first(nz)]
    for device in partners:
        pl.semaphore_signal(barrier, inc=1, device_id=device, device_id_type=MESH)

    loads = [
        pltpu.make_async_copy(source, target, local.at[i])
        for i, (source, target) in enumerate(
            (
                (keys_hbm, keys),
                (values_hbm, values),
                (index_hbm, index),
                (pool_hbm, pool),
                (w_out_hbm, wo_full.at[y]),
                (w_hidden_hbm, wh_full.at[y]),
                (w_query_hbm, w_query),
                (label_hbm, label_ref),
                (gain_hbm, gain_ref),
                (w_logit_hbm, w_logit),
            )
        )
    ]
    for load in loads:
        load.start()
    loads[0].wait()
    loads[1].wait()
    kv_own[...] = jnp.concatenate([keys[...].astype(F32), values[...].astype(F32)], axis=1)
    pl.semaphore_wait(barrier, len(partners))

    hub = z % 2 == c
    kvx_pair, kx_pair, kc_pair = net.pair(), net.pair(), net.pair()
    s_kz, r_kz = net.take(1), net.take(half_z)
    kv_tile = kv_buf.at[c, x, z // 2]

    @pl.when(jnp.logical_not(hub))
    def _():
        net.send(kv_own, kvx, kvx_pair, net.sibling())

    @pl.when(hub)
    def _():
        net.arrived(kvx, kvx_pair[1])
        own, extra = kv_own[...], kvx[...]
        low = jnp.where(c == 0, own, extra)
        high = jnp.where(c == 0, extra, own)
        kv_buf[c, x, z // 2] = jnp.concatenate([low, high], axis=0).astype(BF16)
        for d in far_first(nz):
            net.send(kv_tile, kv_tile, (s_kz, (r_kz, z // 2)), net.z_at(d))

    loads[2].wait()
    loads[3].wait()
    spots = lax.broadcasted_iota(jnp.int32, (pool.shape[1], points), 0)
    chosen = jnp.where(spots == index[...].reshape(1, points), 1.0, 0.0).astype(BF16)
    picked = dot(pool[...], chosen).T.astype(BF16)
    wide, narrow = packed(picked)
    rows_wide[y] = wide
    rows_narrow[y] = narrow

    wide_pair, narrow_pair = net.pair(), net.pair()
    for d in far_first(ny):
        net.send(rows_wide.at[y], rows_wide.at[y], wide_pair, net.y_at(d))
        net.send(rows_narrow.at[y], rows_narrow.at[y], narrow_pair, net.y_at(d))
    others = pl.ds(0, ny - 1)
    net.later(rows_wide.at[others], wide_pair)
    net.later(rows_narrow.at[others], narrow_pair)

    @net.ends.append
    def _():
        @pl.when(hub)
        def _():
            net.sent(gkv_zr, (s_kz, 0))

        @pl.when(jnp.logical_not(hub))
        def _():
            net.sent(kv_own, kvx_pair)

    wo_pair, near_pair, far_pair, wl_pair = net.pair(), net.pair(), net.pair(), net.pair()
    wx_pair, fo_pair, fn_pair, ff_pair = net.pair(), net.pair(), net.pair(), net.pair()
    o_rows, h_rows = wo_full.shape[1] // 2, wh_full.shape[1] // 2
    x_rows = h_rows // NX
    far = ny // 2

    def wo_half(owner, core):
        return wo_full.at[owner, pl.ds(core * o_rows, o_rows)]

    def wh_half(owner, core):
        return wh_full.at[owner, pl.ds(core * h_rows, h_rows)]

    def wh_part(owner, core, part):
        return wh_full.at[owner, pl.ds(core * h_rows + part * x_rows, x_rows)]

    def wo_bytes(count):
        return wo_full.at[pl.ds(0, count), pl.ds(0, o_rows)]

    def wh_bytes(count):
        return wh_full.at[pl.ds(0, count), pl.ds(0, h_rows)]

    loads[4].wait()
    for d in far_first(ny):
        net.send(wo_half(y, c), wo_half(y, c), wo_pair, net.y_at(d))
    net.later(wo_bytes(ny - 1), wo_pair)
    loads[5].wait()
    loads[9].wait()
    wl_full[y] = w_logit[...].astype(F32).reshape(1, hidden)
    for d in far_first(ny):
        if d == far:
            net.send(wh_part(y, c, x), wh_part(y, c, x), far_pair, net.y_at(d))
        else:
            net.send(wh_half(y, c), wh_half(y, c), near_pair, net.y_at(d))
        net.send(wl_full.at[y], wl_full.at[y], wl_pair, net.y_at(d))
    net.later(wh_part(0, 0, 0), far_pair)
    net.later(wh_bytes(ny - 2), near_pair)
    net.later(wl_full.at[others], wl_pair)

    for i in range(half_z):
        tile = kv_buf.at[c, x, i]

        @pl.when(jnp.logical_or(jnp.logical_not(hub), z // 2 != i))
        def _(tile=tile, i=i):
            net.arrived(tile, (r_kz, i))

        if i % 2:
            two = kv_buf.at[c, x, pl.ds(i - 1, 2)]
            for d in far_first(NX):
                net.send(two, two, kx_pair, net.x_at(d))
    net.later(gkv_xr, kx_pair)
    net.arrived(rows_wide.at[others], wide_pair[1])
    net.arrived(rows_narrow.at[others], narrow_pair[1])
    rows_in[...] = jnp.concatenate(
        [unpacked(rows_wide[i], rows_narrow[i]) for i in range(ny)], axis=1
    )
    loads[6].wait()
    query = dot_nt(rows_in[...], w_query[...]).astype(BF16)
    q_ref[...] = query
    own = kv_buf.at[c, x]
    net.send(own, own, kc_pair, net.sibling())
    net.arrived(gkv_xr, kx_pair[1])
    for d in range(1, NX):
        block = kv_buf.at[c, (x + NX - d) % NX]
        net.send(block, block, kc_pair, net.sibling())
    net.later(gkv_xs, kc_pair)
    far_y = (y + ny - far) % ny
    net.arrived(wo_bytes(ny - 1), wo_pair[1])
    for d in range(1, ny):
        block = wo_half((y + ny - d) % ny, c)
        net.send(block, block, fo_pair, net.sibling())
    net.later(wo_bytes(ny - 1), fo_pair)
    net.arrived(wh_part(0, 0, 0), far_pair[1])
    for d in far_first(NX):
        net.send(wh_part(far_y, c, x), wh_part(far_y, c, x), wx_pair, net.x_at(d))
    three = wh_full.at[0, pl.ds(0, (NX - 1) * x_rows)]
    net.later(three, wx_pair)
    net.arrived(gkv_xs, kc_pair[1])

    columns = w_query.shape[0]
    heads = columns // HD
    latents = 16 * half_z * NX * 2
    kv = kv_buf[...].reshape(latents, 2 * columns)
    k_all, v_all = kv[:, :columns], kv[:, columns:]
    kv_t_ref[columns:] = v_all.T
    att_pair = net.pair()
    lane_head = lax.broadcasted_iota(jnp.int32, (points, columns), 1) // HD
    scale = HD ** (-0.5)
    log2e = 1.4426950408889634
    for h in range(heads):
        q_h = jnp.where(lane_head == h, query, jnp.zeros_like(query))
        raw = dot_nt(k_all, q_h)
        top = jnp.max(raw, axis=0, keepdims=True)
        e = jnp.exp2((raw - top) * (scale * log2e))
        p_h = (e * (1.0 / jnp.sum(e, axis=0, keepdims=True))).astype(BF16)
        probs[h] = p_h
        v_t = kv_t_ref[columns + h * HD : columns + (h + 1) * HD]
        att_h = dot(v_t, p_h).astype(BF16)
        att_t[h * HD : (h + 1) * HD] = att_h
        att_buf[y, h] = folded(att_h.T)
        for d in far_first(ny):
            net.send(att_buf.at[y, h], att_buf.at[y, h], att_pair, net.y_at(d))

    net.later(att_buf.at[others], att_pair)
    kv_t_ref[:columns] = k_all.T
    net.arrived(wl_full.at[others], wl_pair[1])
    net.arrived(wh_bytes(ny - 2), near_pair[1])
    for d in range(1, ny):
        if d != far:
            block = wh_half((y + ny - d) % ny, c)
            net.send(block, block, fn_pair, net.sibling())
    net.later(wh_bytes(ny - 2), fn_pair)
    net.arrived(three, wx_pair[1])
    net.send(wh_half(far_y, c), wh_half(far_y, c), ff_pair, net.sibling())
    net.later(wh_half(0, 0), ff_pair)
    net.arrived(wo_bytes(ny - 1), fo_pair[1])
    net.arrived(att_buf.at[others], att_pair[1])

    attended = jnp.concatenate(
        [unfolded(att_buf[i, h]) for i in range(ny) for h in range(heads)], axis=1
    )
    mixed = rows_in[...].astype(F32) + dot(attended, wo_full[...].reshape(width, width))
    center = mixed - jnp.mean(mixed, axis=1, keepdims=True)
    rstd = lax.rsqrt(jnp.mean(center * center, axis=1, keepdims=True) + EPSILON)
    loads[8].wait()
    gain = gain_ref[...].astype(F32).reshape(1, width)
    normal = center * rstd
    normal_ref[...] = normal
    normed_ref[...] = (normal * gain).astype(BF16)

    net.arrived(wh_bytes(ny - 2), fn_pair[1])
    net.arrived(wh_half(0, 0), ff_pair[1])

    root = 0.7978845608028654
    cubic = 0.044715
    logit = jnp.zeros((points, 1), F32)
    for i in range(ny):
        v = dot(normed_ref[...], wh_full[i])
        v2 = v * v
        gate = 0.5 + 0.5 * jnp.tanh(v * (root + (root * cubic) * v2))
        smooth = v * gate
        act = smooth.astype(BF16)
        act_ref[i] = act
        slope_ref[i] = gate + smooth * (1.0 - gate) * (2.0 * root + (6.0 * root * cubic) * v2)
        logit += jnp.sum(act.astype(F32) * wl_full[i], axis=1, keepdims=True)
    total_points = points * nz * NX * NC
    loads[7].wait()
    label = label_ref[...].astype(F32).reshape(1, points)
    label = jnp.broadcast_to(label, (8, points)).T[:, 0:1]
    d_logit = (jax.nn.sigmoid(logit) - label) * total_points ** (-0.5)
    for i in range(ny):
        dh_ref[i] = (d_logit * wl_full[i] * slope_ref[i]).astype(BF16)

    hidden_sum = WeightSum(net, (hid_part, hid_cr, hid_xs, hid_xr, hid_zs, hid_zr, hid_full), False)
    out_sum = WeightSum(net, (out_part, out_cr, out_xs, out_xr, out_zs, out_zr, out_full), True)
    query_sum = WeightSum(net, (que_part, que_cr, que_xs, que_xr, que_zs, que_zr, que_full), False)
    sums = (hidden_sum, out_sum, query_sum)

    normed_t = normed_ref[...].T
    depth = normed_t.shape[0] // 2
    for k in range(2):
        grad = dot(normed_t[k * depth : (k + 1) * depth], dh_ref[y])
        for cc in range(NC):
            for xx in range(NX):
                row = (cc * NX + xx) * 48
                hidden_sum.put(cc, xx, grad[row : row + 48], k)
    hidden_sum.start()
    grad_logit = jnp.sum(d_logit * act_ref[y].astype(F32), axis=0, keepdims=True)

    d_normed = dot_nt(dh_ref[0], wh_full[0])
    for i in range(1, ny):
        d_normed += dot_nt(dh_ref[i], wh_full[i])
    normal = normal_ref[...]
    both = d_normed * normal
    grad_gain = jnp.sum(both, axis=0, keepdims=True)
    scaled = d_normed * gain
    d_mixed = rstd * (
        scaled
        - jnp.mean(scaled, axis=1, keepdims=True)
        - normal * jnp.mean(both * gain, axis=1, keepdims=True)
    )
    d_mixed = d_mixed.astype(BF16)

    hidden_sum.to_x()

    lines = [grad_logit[:, 128 * i : 128 * (i + 1)] for i in range(3)]
    lines += [grad_gain[:, 128 * i : 128 * (i + 1)] for i in range(6)]
    for i in range(NC * NX):
        second = lines[8] if i == 0 else jnp.zeros((1, 128), F32)
        block = jnp.concatenate([lines[i], second, jnp.zeros((14, 128), F32)], axis=0)
        que_part[i // NX, i % NX, 9] = block.astype(BF16)

    def block_rows(chunk, grad):
        for cc in range(NC):
            for xx in range(NX):
                chunk.put(cc, xx, grad[xx * 48 : xx * 48 + 48, cc * 384 : cc * 384 + 384])

    block_rows(out_sum, dot(att_t[...], d_mixed))
    out_sum.start()
    w_out = wo_full[y]
    d_att = dot_nt(d_mixed, w_out).astype(BF16)
    d_att_t = dot_nt(w_out, d_mixed).astype(BF16)

    query = q_ref[...]
    v_all = kv_buf[...].reshape(latents, 2 * columns)[:, columns:]
    d_query = []
    for h in range(heads):
        rows = slice(h * HD, (h + 1) * HD)
        d_att_h = jnp.where(lane_head == h, d_att, jnp.zeros_like(d_att))
        delta = jnp.sum(d_att_t[rows].astype(F32) * att_t[rows].astype(F32), axis=0, keepdims=True)
        d_probs = dot_nt(v_all, d_att_h)
        d_scores = (probs[h].astype(F32) * (d_probs - delta) * scale).astype(BF16)
        ds_ref[h] = d_scores
        d_query.append(dot(kv_t_ref[rows], d_scores).astype(BF16))
        if h == 0:
            out_sum.to_x()
    block_rows(query_sum, dot(jnp.concatenate(d_query, axis=0), rows_in[...]))
    query_sum.start()
    hidden_sum.to_z()

    grad_k = jnp.zeros((latents, columns), F32)
    grad_v = jnp.zeros((latents, columns), F32)
    for h in range(heads):
        d_att_h = jnp.where(lane_head == h, d_att, jnp.zeros_like(d_att))
        q_h = jnp.where(lane_head == h, query, jnp.zeros_like(query))
        grad_k += dot(ds_ref[h], q_h)
        grad_v += dot(probs[h], d_att_h)
        if h == 0:
            query_sum.to_x()
            out_sum.to_z()
    grads = jnp.concatenate([grad_k, grad_v], axis=1).astype(BF16)
    gkv[...] = grads.reshape(gkv.shape)
    gc_pair, gx_pair, gz_pair, gf_pair = net.pair(), net.pair(), net.pair(), net.pair()
    net.send(gkv.at[other], gkv_cr, gc_pair, net.sibling())
    net.later(gkv_cr, gc_pair)

    net.arrived(gkv_cr, gc_pair[1])
    gkv_xs[...] = (gkv[c].astype(F32) + gkv_cr[...].astype(F32)).astype(BF16)
    for d in far_first(NX):
        net.send(gkv_xs.at[(x + d) % NX], gkv_xr.at[d - 1], gx_pair, net.x_at(d))
    net.later(gkv_xr, gx_pair)

    query_sum.to_z()
    hidden_sum.back_z()
    out_sum.back_z()
    query_sum.back_z()

    hidden_sum.back_x()
    total = gkv_xs[x].astype(F32)
    net.arrived(gkv_xr, gx_pair[1])
    for d in range(1, NX):
        total += gkv_xr[d - 1].astype(F32)
    gkv_zs[...] = total.astype(BF16)
    for d in far_first(nz):
        target = (z + d) % nz

        @pl.when(target % 2 == c)
        def _(d=d, target=target):
            net.send(gkv_zs.at[target // 2], gkv_zr.at[d - 1], gz_pair, net.at(z=target))

    @net.ends.append
    def _():
        @pl.when(hub)
        def _():
            net.sent(gkv_zs.at[pl.ds(0, half_z - 1)], gz_pair)

        @pl.when(jnp.logical_not(hub))
        def _():
            net.sent(gkv_zs, gz_pair)

    out_sum.back_x()
    query_sum.back_x()

    hidden_sum.back_core()
    out_sum.back_core()
    @pl.when(hub)
    def _():
        net.arrived(gkv_zr, gz_pair[1])
        total = gkv_zs[z // 2].astype(F32)
        for d in range(1, nz):
            total += gkv_zr[d - 1].astype(F32)
        gkv_sum[...] = total.reshape(gkv_sum.shape)
        net.send(gkv_sum.at[other], okv_ref, gf_pair, net.sibling())
        okv_ref[...] = gkv_sum[c]

    @net.ends.append
    def _():
        @pl.when(hub)
        def _():
            net.sent(gkv_sum.at[other], gf_pair)

    query_sum.back_core()

    @pl.when(jnp.logical_not(hub))
    def _():
        net.arrived(okv_ref, gf_pair[1])

    stores = [pltpu.make_async_copy(okv_ref, okv_hbm, local.at[10])]
    stores[0].start()
    places = ((hid_full, hid_hbm), (out_full, out_hbm), (que_full, que_hbm))
    for i, (chunk, (held, target)) in enumerate(zip(sums, places)):
        chunk.end()
        stores.append(pltpu.make_async_copy(held, target, local.at[11 + i]))
        stores[-1].start()
    for store in stores:
        store.wait()
    net.finish()
    assert net.used <= SEMAPHORES, net.used


def write_kernel(
    hid_hbm,
    out_hbm,
    que_hbm,
    kv_hbm,
    wq_ref,
    wo_ref,
    wh_ref,
    logit_ref,
    gain_ref,
    keys_ref,
    values_ref,
    hid_ref,
    out_ref,
    que_ref,
    kv_ref,
    sems,
):
    pairs = ((hid_hbm, hid_ref), (out_hbm, out_ref), (que_hbm, que_ref), (kv_hbm, kv_ref))
    loads = [pltpu.make_async_copy(a, b, sems.at[i]) for i, (a, b) in enumerate(pairs)]
    for load in loads:
        load.start()

    def block(ref, c, x, slot=0):
        rows = []
        for r in range(3):
            tiles = [ref[c, x, 3 * r + l, 16 * slot : 16 * slot + 16] for l in range(3)]
            rows.append(jnp.concatenate(tiles, axis=1))
        return jnp.concatenate(rows, axis=0).astype(F32)

    depth = wh_ref.shape[0] // 2
    parts = [(c, x) for c in range(NC) for x in range(NX)]
    loads[0].wait()
    for slot in range(2):
        for c, x in parts:
            row = slot * depth + (c * NX + x) * 48
            wh_ref[row : row + 48, :] = block(hid_ref, c, x, slot)
    for load, source, target in ((loads[1], out_ref, wo_ref), (loads[2], que_ref, wq_ref)):
        load.wait()
        for c, x in parts:
            target[x * 48 : x * 48 + 48, c * 384 : c * 384 + 384] = block(source, c, x)
    vectors = [que_ref[c, x, 9].astype(F32) for c, x in parts]
    lines = [vector[0:1] for vector in vectors] + [vectors[0][1:2]]
    for i in range(3):
        logit_ref[128 * i : 128 * (i + 1)] = lines[i].reshape(128)
    for i in range(6):
        gain_ref[128 * i : 128 * (i + 1)] = lines[3 + i].reshape(128)
    loads[3].wait()
    columns = keys_ref.shape[1]
    keys_ref[...] = kv_ref[:, :columns]
    values_ref[...] = kv_ref[:, columns:]


def solution(mesh):
    nz = mesh.shape["pts"] // (NX * NC)
    ny = mesh.shape["head"]
    half_z = nz // 2

    def on_device(pool, index, labels, w_query, keys, values, w_out, out_gain, w_hidden, w_logit):
        points, columns = index.shape[0], keys.shape[1]
        width, hidden = w_hidden.shape
        latents = keys.shape[0] * nz * NX * NC
        heads = columns // HD
        vmem = pltpu.VMEM
        wide = (16, 2 * columns)
        forms = ((9, (32, 128)), (9, (16, 128)), (10, (16, 128)))
        shapes = [
            jax.ShapeDtypeStruct((NC, NX, count) + tile, BF16) for count, tile in forms
        ] + [jax.ShapeDtypeStruct((8, 2 * columns), F32)]
        buffers = []
        for count, tile in forms:
            buffers += [
                vmem((NC, NX, count) + tile, BF16),
                vmem((NX, count) + tile, BF16),
                vmem((NX, count) + tile, BF16),
                vmem((NX - 1, count) + tile, BF16),
                vmem((count,) + tile, BF16),
                vmem((nz - 1,) + tile, BF16),
            ]
        scratch = [vmem(shape.shape, shape.dtype) for shape in shapes] + [
            vmem((columns, pool.shape[0]), BF16),
            vmem((points,), jnp.int32),
            vmem((points,), jnp.int32),
            vmem((width,), BF16),
            vmem((hidden,), BF16),
            vmem((columns, width), BF16),
            vmem(keys.shape, BF16),
            vmem(keys.shape, BF16),
            vmem((ny, points, 128), BF16),
            vmem((ny, points // 2, 128), BF16),
            vmem((points, width), BF16),
            vmem((ny, columns, width), BF16),
            vmem((ny, width, hidden), BF16),
            vmem((ny, 1, hidden), F32),
            vmem((8, 2 * columns), F32),
            vmem((8, 2 * columns), F32),
            vmem((2, NX, half_z) + wide, BF16),
            vmem((points, columns), BF16),
            vmem((heads, latents, points), BF16),
            vmem((columns, points), BF16),
            vmem((ny, heads, points // 2, 128), BF16),
            vmem((2 * columns, latents), BF16),
            vmem((heads, latents, points), BF16),
            vmem((points, width), F32),
            vmem((points, width), BF16),
            vmem((ny, points, hidden), BF16),
            vmem((ny, points, hidden), F32),
            vmem((ny, points, hidden), BF16),
            *buffers,
            vmem((2, NX, half_z) + wide, BF16),
            vmem((NX, half_z) + wide, BF16),
            vmem((NX, half_z) + wide, BF16),
            vmem((NX - 1, half_z) + wide, BF16),
            vmem((half_z,) + wide, BF16),
            vmem((nz - 1,) + wide, BF16),
            vmem((2, 8, 2 * columns), F32),
            pltpu.SemaphoreType.DMA((16,)),
            pltpu.SemaphoreType.DMA((SEMAPHORES,)),
        ]
        whole = pl.BlockSpec(memory_space=pltpu.VMEM)
        sums = pl.pallas_call(
            lambda *refs: kernel(nz, ny, *refs),
            out_shape=shapes,
            in_specs=[pl.BlockSpec(memory_space=pl.ANY)] * 10,
            out_specs=[pl.BlockSpec(memory_space=pl.ANY)] * 4,
            scratch_shapes=scratch,
            compiler_params=pltpu.CompilerParams(
                collective_id=0, has_side_effects=True, vmem_limit_bytes=56 * 1024 * 1024
            ),
        )(pool.T, index, labels, out_gain, w_logit, w_query.T, keys, values, w_out, w_hidden)
        outs = pl.pallas_call(
            write_kernel,
            out_shape=[
                jax.ShapeDtypeStruct((columns, width), F32),
                jax.ShapeDtypeStruct((columns, width), F32),
                jax.ShapeDtypeStruct((width, hidden), F32),
                jax.ShapeDtypeStruct((hidden,), F32),
                jax.ShapeDtypeStruct((width,), F32),
                jax.ShapeDtypeStruct(keys.shape, F32),
                jax.ShapeDtypeStruct(keys.shape, F32),
            ],
            in_specs=[pl.BlockSpec(memory_space=pltpu.HBM)] * 4,
            out_specs=[whole] * 7,
            scratch_shapes=[vmem(shape.shape, shape.dtype) for shape in shapes]
            + [pltpu.SemaphoreType.DMA((4,))],
            compiler_params=pltpu.CompilerParams(vmem_limit_bytes=60 * 1024 * 1024),
        )(*sums)
        return (outs[0].T,) + tuple(outs[1:])

    return jax.shard_map(
        on_device,
        mesh=mesh,
        in_specs=(
            P("pts", "head"),
            P("pts"),
            P("pts"),
            P(None, "head"),
            P("pts", "head"),
            P("pts", "head"),
            P("head", None),
            P(),
            P(None, "head"),
            P("head"),
        ),
        out_specs=(
            P(None, "head"),
            P("head", None),
            P(None, "head"),
            P("head"),
            P(),
            P("pts", "head"),
            P("pts", "head"),
        ),
        check_vma=False,
    )
```

```python
import jax
import jax.numpy as jnp
from jax import lax
from jax.experimental import pallas as pl
from jax.experimental.pallas import tpu as pltpu
from jax.sharding import PartitionSpec as P

HD = 64
EPSILON = 1e-05
NX = 4
NC = 2
SEMAPHORES = 96
MESH = pl.DeviceIdType.MESH
F32 = jnp.float32
BF16 = jnp.bfloat16


def dot(a, b):
    return jnp.dot(a, b, preferred_element_type=F32)


def dot_nt(a, b):
    return lax.dot_general(a, b, (((1,), (1,)), ((), ())), preferred_element_type=F32)


def far_first(n):
    return sorted(range(1, n), key=lambda d: -min(d, n - d))


def packed(block):
    half = block.shape[0] // 2
    return block[:, :128], jnp.concatenate([block[:half, 128:], block[half:, 128:]], axis=1)


def folded(block):
    half = block.shape[0] // 2
    return jnp.concatenate([block[:half], block[half:]], axis=1)


def unfolded(block):
    return jnp.concatenate([block[:, :64], block[:, 64:]], axis=0)


def unpacked(wide, narrow):
    return jnp.concatenate([wide, jnp.concatenate([narrow[:, :64], narrow[:, 64:]], axis=0)], axis=1)


class Links:
    def __init__(self, nz, ny, sems):
        self.nz, self.ny, self.sems, self.used = nz, ny, sems, 0
        p = lax.axis_index("pts")
        self.y = lax.axis_index("head")
        self.c = p % NC
        self.x = (p // NC) % NX
        self.z = p // (NC * NX)
        self.other = 1 - self.c
        self.ends = []

    def at(self, x=None, y=None, z=None, c=None):
        x = self.x if x is None else x
        y = self.y if y is None else y
        z = self.z if z is None else z
        c = self.c if c is None else c
        return (z * (NC * NX) + x * NC + c, y)

    def x_at(self, d):
        return self.at(x=(self.x + d) % NX)

    def y_at(self, d):
        return self.at(y=(self.y + d) % self.ny)

    def z_at(self, d):
        return self.at(z=(self.z + d) % self.nz)

    def sibling(self):
        return self.at(c=self.other)

    def take(self, count):
        first = self.used
        self.used += count
        return first

    def copy(self, src, dst, send, recv, device):
        return pltpu.make_async_remote_copy(
            src_ref=src,
            dst_ref=dst,
            send_sem=self.sems.at[send],
            recv_sem=self.sems.at[recv if isinstance(recv, int) else sum(recv)],
            device_id=device,
            device_id_type=MESH,
        )

    def pair(self):
        return self.take(1), self.take(1)

    def send(self, src, dst, pair, device):
        self.copy(src, dst, pair[0], pair[1], device).start()

    def arrived(self, total, recv):
        self.copy(total, total, 0, recv, self.sibling()).wait_recv()

    def sent(self, total, pair):
        self.copy(total, total, pair[0], 0, self.sibling()).wait_send()

    def later(self, total, pair):
        self.ends.append(lambda: self.sent(total, pair))

    def finish(self):
        for end in self.ends:
            end()


class WeightSum:
    def __init__(self, net, refs, mirrored):
        self.net, self.mirrored = net, mirrored
        self.part, self.cr, self.xs, self.xr, self.zs, self.zr, self.full = refs
        self.count = self.zs.shape[0]
        self.core, self.x, self.z = net.pair(), net.pair(), net.pair()
        self.gz, self.gx, self.gc = net.pair(), net.pair(), net.pair()
        self.piece, self.reduces = self.role(net.z)

    def role(self, z):
        nz = self.net.nz
        spot = (nz - 1 - z) if self.mirrored else z
        piece = (self.count * spot + nz - 1) // nz
        return jnp.minimum(piece, self.count - 1), (nz * piece) // self.count == spot

    def put(self, c, x, block, slot=0):
        block = block.astype(BF16)
        for j in range(9):
            r, l = 16 * (j // 3), 128 * (j % 3)
            self.part[c, x, j, 16 * slot : 16 * slot + 16] = block[r : r + 16, l : l + 128]

    def start(self):
        net = self.net
        net.send(self.part.at[net.other], self.cr, self.core, net.sibling())
        net.later(self.cr, self.core)

    def to_x(self):
        net = self.net
        net.arrived(self.cr, self.core[1])
        self.xs[...] = (self.part[net.c].astype(F32) + self.cr[...].astype(F32)).astype(BF16)
        for d in far_first(NX):
            target = (net.x + d) % NX
            net.send(self.xs.at[target], self.xr.at[d - 1], self.x, net.x_at(d))
        net.later(self.xr, self.x)

    def to_z(self):
        net = self.net
        net.arrived(self.xr, self.x[1])
        total = self.xs[net.x].astype(F32)
        for d in range(1, NX):
            total += self.xr[d - 1].astype(F32)
        self.zs[...] = total.astype(BF16)
        for d in far_first(net.nz):
            spot = (net.z + d) % net.nz
            piece, reduces = self.role(spot)

            @pl.when(reduces)
            def _(d=d, piece=piece, spot=spot):
                net.send(self.zs.at[piece], self.zr.at[d - 1], self.z, net.at(z=spot))

        @net.ends.append
        def _():
            self.pieces(lambda total: net.sent(total, self.z))

    def pieces(self, wait):
        @pl.when(self.reduces)
        def _():
            wait(self.zs.at[pl.ds(0, self.count - 1)])

        @pl.when(jnp.logical_not(self.reduces))
        def _():
            wait(self.zs)

    def back_z(self):
        net = self.net
        tile = self.full.at[net.c, net.x, self.piece]

        @pl.when(self.reduces)
        def _():
            net.arrived(self.zr, self.z[1])
            total = self.zs[self.piece].astype(F32)
            for d in range(1, net.nz):
                total += self.zr[d - 1].astype(F32)
            self.full[net.c, net.x, self.piece] = total.astype(BF16)
            for d in far_first(net.nz):
                net.send(tile, tile, self.gz, net.z_at(d))

        @net.ends.append
        def _():
            @pl.when(self.reduces)
            def _():
                net.sent(self.zr, self.gz)

    def back_x(self):
        net = self.net
        self.pieces(lambda total: net.arrived(total, self.gz[1]))
        mine = self.full.at[net.c, net.x]
        for d in far_first(NX):
            net.send(mine, mine, self.gx, net.x_at(d))
        net.later(self.xr, self.gx)

    def back_core(self):
        net = self.net
        net.arrived(self.xr, self.gx[1])
        mine = self.full.at[net.c]
        net.send(mine, mine, self.gc, net.sibling())
        net.later(mine, self.gc)

    def end(self):
        net = self.net
        net.arrived(self.full.at[net.other], self.gc[1])


def kernel(
    nz,
    ny,
    pool_hbm,
    index_hbm,
    label_hbm,
    gain_hbm,
    w_logit_hbm,
    w_query_hbm,
    keys_hbm,
    values_hbm,
    w_out_hbm,
    w_hidden_hbm,
    hid_hbm,
    out_hbm,
    que_hbm,
    okv_hbm,
    hid_full,
    out_full,
    que_full,
    okv_ref,
    pool,
    index,
    label_ref,
    gain_ref,
    w_logit,
    w_query,
    keys,
    values,
    rows_wide,
    rows_narrow,
    rows_in,
    wo_full,
    wh_full,
    wl_full,
    kv_own,
    kvx,
    kv_buf,
    q_ref,
    probs,
    att_t,
    att_buf,
    kv_t_ref,
    ds_ref,
    normal_ref,
    normed_ref,
    act_ref,
    slope_ref,
    dh_ref,
    hid_part,
    hid_cr,
    hid_xs,
    hid_xr,
    hid_zs,
    hid_zr,
    out_part,
    out_cr,
    out_xs,
    out_xr,
    out_zs,
    out_zr,
    que_part,
    que_cr,
    que_xs,
    que_xr,
    que_zs,
    que_zr,
    gkv,
    gkv_cr,
    gkv_xs,
    gkv_xr,
    gkv_zs,
    gkv_zr,
    gkv_sum,
    local,
    sems,
):
    net = Links(nz, ny, sems)
    x, y, z, c, other = net.x, net.y, net.z, net.c, net.other
    points, width = rows_in.shape
    half_z = nz // 2
    hidden = wh_full.shape[2]

    barrier = pltpu.get_barrier_semaphore()
    partners = [net.sibling()]
    partners += [net.x_at(d) for d in range(1, NX)]
    partners += [net.y_at(d) for d in range(1, ny)]
    partners += [net.z_at(d) for d in far_first(nz)]
    for device in partners:
        pl.semaphore_signal(barrier, inc=1, device_id=device, device_id_type=MESH)

    loads = [
        pltpu.make_async_copy(source, target, local.at[i])
        for i, (source, target) in enumerate(
            (
                (keys_hbm, keys),
                (values_hbm, values),
                (index_hbm, index),
                (pool_hbm, pool),
                (w_out_hbm, wo_full.at[y]),
                (w_hidden_hbm, wh_full.at[y]),
                (w_query_hbm, w_query),
                (label_hbm, label_ref),
                (gain_hbm, gain_ref),
                (w_logit_hbm, w_logit),
            )
        )
    ]
    for load in loads:
        load.start()
    loads[0].wait()
    loads[1].wait()
    kv_own[...] = jnp.concatenate([keys[...].astype(F32), values[...].astype(F32)], axis=1)
    pl.semaphore_wait(barrier, len(partners))

    hub = z % 2 == c
    kvx_pair, kx_pair, kc_pair = net.pair(), net.pair(), net.pair()
    s_kz, r_kz = net.take(1), net.take(half_z)
    kv_tile = kv_buf.at[c, x, z // 2]

    @pl.when(jnp.logical_not(hub))
    def _():
        net.send(kv_own, kvx, kvx_pair, net.sibling())

    @pl.when(hub)
    def _():
        net.arrived(kvx, kvx_pair[1])
        own, extra = kv_own[...], kvx[...]
        low = jnp.where(c == 0, own, extra)
        high = jnp.where(c == 0, extra, own)
        kv_buf[c, x, z // 2] = jnp.concatenate([low, high], axis=0).astype(BF16)
        for d in far_first(nz):
            net.send(kv_tile, kv_tile, (s_kz, (r_kz, z // 2)), net.z_at(d))

    loads[2].wait()
    loads[3].wait()
    spots = lax.broadcasted_iota(jnp.int32, (pool.shape[1], points), 0)
    chosen = jnp.where(spots == index[...].reshape(1, points), 1.0, 0.0).astype(BF16)
    picked = dot(pool[...], chosen).T.astype(BF16)
    wide, narrow = packed(picked)
    rows_wide[y] = wide
    rows_narrow[y] = narrow

    wide_pair, narrow_pair = net.pair(), net.pair()
    for d in far_first(ny):
        net.send(rows_wide.at[y], rows_wide.at[y], wide_pair, net.y_at(d))
        net.send(rows_narrow.at[y], rows_narrow.at[y], narrow_pair, net.y_at(d))
    others = pl.ds(0, ny - 1)
    net.later(rows_wide.at[others], wide_pair)
    net.later(rows_narrow.at[others], narrow_pair)

    @net.ends.append
    def _():
        @pl.when(hub)
        def _():
            net.sent(gkv_zr, (s_kz, 0))

        @pl.when(jnp.logical_not(hub))
        def _():
            net.sent(kv_own, kvx_pair)

    wo_pair, near_pair, far_pair, wl_pair = net.pair(), net.pair(), net.pair(), net.pair()
    wx_pair, fo_pair, fn_pair, ff_pair = net.pair(), net.pair(), net.pair(), net.pair()
    o_rows, h_rows = wo_full.shape[1] // 2, wh_full.shape[1] // 2
    x_rows = h_rows // NX
    far = ny // 2

    def wo_half(owner, core):
        return wo_full.at[owner, pl.ds(core * o_rows, o_rows)]

    def wh_half(owner, core):
        return wh_full.at[owner, pl.ds(core * h_rows, h_rows)]

    def wh_part(owner, core, part):
        return wh_full.at[owner, pl.ds(core * h_rows + part * x_rows, x_rows)]

    def wo_bytes(count):
        return wo_full.at[pl.ds(0, count), pl.ds(0, o_rows)]

    def wh_bytes(count):
        return wh_full.at[pl.ds(0, count), pl.ds(0, h_rows)]

    loads[4].wait()
    for d in far_first(ny):
        net.send(wo_half(y, c), wo_half(y, c), wo_pair, net.y_at(d))
    net.later(wo_bytes(ny - 1), wo_pair)
    loads[5].wait()
    loads[9].wait()
    wl_full[y] = w_logit[...].astype(F32).reshape(1, hidden)
    for d in far_first(ny):
        if d == far:
            net.send(wh_part(y, c, x), wh_part(y, c, x), far_pair, net.y_at(d))
        else:
            net.send(wh_half(y, c), wh_half(y, c), near_pair, net.y_at(d))
        net.send(wl_full.at[y], wl_full.at[y], wl_pair, net.y_at(d))
    net.later(wh_part(0, 0, 0), far_pair)
    net.later(wh_bytes(ny - 2), near_pair)
    net.later(wl_full.at[others], wl_pair)

    for i in range(half_z):
        tile = kv_buf.at[c, x, i]

        @pl.when(jnp.logical_or(jnp.logical_not(hub), z // 2 != i))
        def _(tile=tile, i=i):
            net.arrived(tile, (r_kz, i))

        if i % 2:
            two = kv_buf.at[c, x, pl.ds(i - 1, 2)]
            for d in far_first(NX):
                net.send(two, two, kx_pair, net.x_at(d))
    net.later(gkv_xr, kx_pair)
    net.arrived(rows_wide.at[others], wide_pair[1])
    net.arrived(rows_narrow.at[others], narrow_pair[1])
    rows_in[...] = jnp.concatenate(
        [unpacked(rows_wide[i], rows_narrow[i]) for i in range(ny)], axis=1
    )
    loads[6].wait()
    query = dot_nt(rows_in[...], w_query[...]).astype(BF16)
    q_ref[...] = query
    own = kv_buf.at[c, x]
    net.send(own, own, kc_pair, net.sibling())
    net.arrived(gkv_xr, kx_pair[1])
    for d in range(1, NX):
        block = kv_buf.at[c, (x + NX - d) % NX]
        net.send(block, block, kc_pair, net.sibling())
    net.later(gkv_xs, kc_pair)
    far_y = (y + ny - far) % ny
    net.arrived(wo_bytes(ny - 1), wo_pair[1])
    for d in range(1, ny):
        block = wo_half((y + ny - d) % ny, c)
        net.send(block, block, fo_pair, net.sibling())
    net.later(wo_bytes(ny - 1), fo_pair)
    net.arrived(wh_part(0, 0, 0), far_pair[1])
    for d in far_first(NX):
        net.send(wh_part(far_y, c, x), wh_part(far_y, c, x), wx_pair, net.x_at(d))
    three = wh_full.at[0, pl.ds(0, (NX - 1) * x_rows)]
    net.later(three, wx_pair)
    net.arrived(gkv_xs, kc_pair[1])

    columns = w_query.shape[0]
    heads = columns // HD
    latents = 16 * half_z * NX * 2
    kv = kv_buf[...].reshape(latents, 2 * columns)
    k_all, v_all = kv[:, :columns], kv[:, columns:]
    kv_t_ref[columns:] = v_all.T
    att_pair = net.pair()
    lane_head = lax.broadcasted_iota(jnp.int32, (points, columns), 1) // HD
    scale = HD ** (-0.5)
    log2e = 1.4426950408889634
    for h in range(heads):
        q_h = jnp.where(lane_head == h, query, jnp.zeros_like(query))
        raw = dot_nt(k_all, q_h)
        top = jnp.max(raw, axis=0, keepdims=True)
        e = jnp.exp2((raw - top) * (scale * log2e))
        p_h = (e * (1.0 / jnp.sum(e, axis=0, keepdims=True))).astype(BF16)
        probs[h] = p_h
        v_t = kv_t_ref[columns + h * HD : columns + (h + 1) * HD]
        att_h = dot(v_t, p_h).astype(BF16)
        att_t[h * HD : (h + 1) * HD] = att_h
        att_buf[y, h] = folded(att_h.T)
        for d in far_first(ny):
            net.send(att_buf.at[y, h], att_buf.at[y, h], att_pair, net.y_at(d))

    net.later(att_buf.at[others], att_pair)
    kv_t_ref[:columns] = k_all.T
    net.arrived(wl_full.at[others], wl_pair[1])
    net.arrived(wh_bytes(ny - 2), near_pair[1])
    for d in range(1, ny):
        if d != far:
            block = wh_half((y + ny - d) % ny, c)
            net.send(block, block, fn_pair, net.sibling())
    net.later(wh_bytes(ny - 2), fn_pair)
    net.arrived(three, wx_pair[1])
    net.send(wh_half(far_y, c), wh_half(far_y, c), ff_pair, net.sibling())
    net.later(wh_half(0, 0), ff_pair)
    net.arrived(wo_bytes(ny - 1), fo_pair[1])
    net.arrived(att_buf.at[others], att_pair[1])

    attended = jnp.concatenate(
        [unfolded(att_buf[i, h]) for i in range(ny) for h in range(heads)], axis=1
    )
    mixed = rows_in[...].astype(F32) + dot(attended, wo_full[...].reshape(width, width))
    center = mixed - jnp.mean(mixed, axis=1, keepdims=True)
    rstd = lax.rsqrt(jnp.mean(center * center, axis=1, keepdims=True) + EPSILON)
    loads[8].wait()
    gain = gain_ref[...].astype(F32).reshape(1, width)
    normal = center * rstd
    normal_ref[...] = normal
    normed_ref[...] = (normal * gain).astype(BF16)

    net.arrived(wh_bytes(ny - 2), fn_pair[1])
    net.arrived(wh_half(0, 0), ff_pair[1])

    root = 0.7978845608028654
    cubic = 0.044715
    logit = jnp.zeros((points, 1), F32)
    for i in range(ny):
        v = dot(normed_ref[...], wh_full[i])
        v2 = v * v
        gate = 0.5 + 0.5 * jnp.tanh(v * (root + (root * cubic) * v2))
        smooth = v * gate
        act = smooth.astype(BF16)
        act_ref[i] = act
        slope_ref[i] = gate + smooth * (1.0 - gate) * (2.0 * root + (6.0 * root * cubic) * v2)
        logit += jnp.sum(act.astype(F32) * wl_full[i], axis=1, keepdims=True)
    total_points = points * nz * NX * NC
    loads[7].wait()
    label = label_ref[...].astype(F32).reshape(1, points)
    label = jnp.broadcast_to(label, (8, points)).T[:, 0:1]
    d_logit = (jax.nn.sigmoid(logit) - label) * total_points ** (-0.5)
    for i in range(ny):
        dh_ref[i] = (d_logit * wl_full[i] * slope_ref[i]).astype(BF16)

    hidden_sum = WeightSum(net, (hid_part, hid_cr, hid_xs, hid_xr, hid_zs, hid_zr, hid_full), False)
    out_sum = WeightSum(net, (out_part, out_cr, out_xs, out_xr, out_zs, out_zr, out_full), True)
    query_sum = WeightSum(net, (que_part, que_cr, que_xs, que_xr, que_zs, que_zr, que_full), False)
    sums = (hidden_sum, out_sum, query_sum)

    normed_t = normed_ref[...].T
    depth = normed_t.shape[0] // 2
    for k in range(2):
        grad = dot(normed_t[k * depth : (k + 1) * depth], dh_ref[y])
        for cc in range(NC):
            for xx in range(NX):
                row = (cc * NX + xx) * 48
                hidden_sum.put(cc, xx, grad[row : row + 48], k)
    hidden_sum.start()
    grad_logit = jnp.sum(d_logit * act_ref[y].astype(F32), axis=0, keepdims=True)

    d_normed = dot_nt(dh_ref[0], wh_full[0])
    for i in range(1, ny):
        d_normed += dot_nt(dh_ref[i], wh_full[i])
    normal = normal_ref[...]
    both = d_normed * normal
    grad_gain = jnp.sum(both, axis=0, keepdims=True)
    scaled = d_normed * gain
    d_mixed = rstd * (
        scaled
        - jnp.mean(scaled, axis=1, keepdims=True)
        - normal * jnp.mean(both * gain, axis=1, keepdims=True)
    )
    d_mixed = d_mixed.astype(BF16)

    hidden_sum.to_x()

    lines = [grad_logit[:, 128 * i : 128 * (i + 1)] for i in range(3)]
    lines += [grad_gain[:, 128 * i : 128 * (i + 1)] for i in range(6)]
    for i in range(NC * NX):
        second = lines[8] if i == 0 else jnp.zeros((1, 128), F32)
        block = jnp.concatenate([lines[i], second, jnp.zeros((14, 128), F32)], axis=0)
        que_part[i // NX, i % NX, 9] = block.astype(BF16)

    def block_rows(chunk, grad):
        for cc in range(NC):
            for xx in range(NX):
                chunk.put(cc, xx, grad[xx * 48 : xx * 48 + 48, cc * 384 : cc * 384 + 384])

    block_rows(out_sum, dot(att_t[...], d_mixed))
    out_sum.start()
    w_out = wo_full[y]
    d_att = dot_nt(d_mixed, w_out).astype(BF16)
    d_att_t = dot_nt(w_out, d_mixed).astype(BF16)

    query = q_ref[...]
    v_all = kv_buf[...].reshape(latents, 2 * columns)[:, columns:]
    d_query = []
    for h in range(heads):
        rows = slice(h * HD, (h + 1) * HD)
        d_att_h = jnp.where(lane_head == h, d_att, jnp.zeros_like(d_att))
        delta = jnp.sum(d_att_t[rows].astype(F32) * att_t[rows].astype(F32), axis=0, keepdims=True)
        d_probs = dot_nt(v_all, d_att_h)
        d_scores = (probs[h].astype(F32) * (d_probs - delta) * scale).astype(BF16)
        ds_ref[h] = d_scores
        d_query.append(dot(kv_t_ref[rows], d_scores).astype(BF16))
        if h == 0:
            out_sum.to_x()
    block_rows(query_sum, dot(jnp.concatenate(d_query, axis=0), rows_in[...]))
    query_sum.start()
    hidden_sum.to_z()

    grad_k = jnp.zeros((latents, columns), F32)
    grad_v = jnp.zeros((latents, columns), F32)
    for h in range(heads):
        d_att_h = jnp.where(lane_head == h, d_att, jnp.zeros_like(d_att))
        q_h = jnp.where(lane_head == h, query, jnp.zeros_like(query))
        grad_k += dot(ds_ref[h], q_h)
        grad_v += dot(probs[h], d_att_h)
        if h == 0:
            query_sum.to_x()
            out_sum.to_z()
    grads = jnp.concatenate([grad_k, grad_v], axis=1).astype(BF16)
    gkv[...] = grads.reshape(gkv.shape)
    gc_pair, gx_pair, gz_pair, gf_pair = net.pair(), net.pair(), net.pair(), net.pair()
    net.send(gkv.at[other], gkv_cr, gc_pair, net.sibling())
    net.later(gkv_cr, gc_pair)

    net.arrived(gkv_cr, gc_pair[1])
    gkv_xs[...] = (gkv[c].astype(F32) + gkv_cr[...].astype(F32)).astype(BF16)
    for d in far_first(NX):
        net.send(gkv_xs.at[(x + d) % NX], gkv_xr.at[d - 1], gx_pair, net.x_at(d))
    net.later(gkv_xr, gx_pair)

    query_sum.to_z()
    hidden_sum.back_z()
    out_sum.back_z()
    query_sum.back_z()

    hidden_sum.back_x()
    total = gkv_xs[x].astype(F32)
    net.arrived(gkv_xr, gx_pair[1])
    for d in range(1, NX):
        total += gkv_xr[d - 1].astype(F32)
    gkv_zs[...] = total.astype(BF16)
    for d in far_first(nz):
        target = (z + d) % nz

        @pl.when(target % 2 == c)
        def _(d=d, target=target):
            net.send(gkv_zs.at[target // 2], gkv_zr.at[d - 1], gz_pair, net.at(z=target))

    @net.ends.append
    def _():
        @pl.when(hub)
        def _():
            net.sent(gkv_zs.at[pl.ds(0, half_z - 1)], gz_pair)

        @pl.when(jnp.logical_not(hub))
        def _():
            net.sent(gkv_zs, gz_pair)

    out_sum.back_x()
    query_sum.back_x()

    for chunk in sums:
        chunk.back_core()
    @pl.when(hub)
    def _():
        net.arrived(gkv_zr, gz_pair[1])
        total = gkv_zs[z // 2].astype(F32)
        for d in range(1, nz):
            total += gkv_zr[d - 1].astype(F32)
        gkv_sum[...] = total.reshape(gkv_sum.shape)
        net.send(gkv_sum.at[other], okv_ref, gf_pair, net.sibling())
        okv_ref[...] = gkv_sum[c]

    @net.ends.append
    def _():
        @pl.when(hub)
        def _():
            net.sent(gkv_sum.at[other], gf_pair)

    stores = []
    places = ((hid_full, hid_hbm), (out_full, out_hbm), (que_full, que_hbm))
    for i, (chunk, (held, target)) in enumerate(zip(sums, places)):
        chunk.end()
        stores.append(pltpu.make_async_copy(held, target, local.at[11 + i]))
        stores[-1].start()

    @pl.when(jnp.logical_not(hub))
    def _():
        net.arrived(okv_ref, gf_pair[1])

    stores.append(pltpu.make_async_copy(okv_ref, okv_hbm, local.at[10]))
    stores[-1].start()
    for store in stores:
        store.wait()
    net.finish()
    assert net.used <= SEMAPHORES, net.used


def write_kernel(
    hid_hbm,
    out_hbm,
    que_hbm,
    kv_hbm,
    wq_ref,
    wo_ref,
    wh_ref,
    logit_ref,
    gain_ref,
    keys_ref,
    values_ref,
    hid_ref,
    out_ref,
    que_ref,
    kv_ref,
    sems,
):
    pairs = ((hid_hbm, hid_ref), (out_hbm, out_ref), (que_hbm, que_ref), (kv_hbm, kv_ref))
    loads = [pltpu.make_async_copy(a, b, sems.at[i]) for i, (a, b) in enumerate(pairs)]
    for load in loads:
        load.start()

    def block(ref, c, x, slot=0):
        rows = []
        for r in range(3):
            tiles = [ref[c, x, 3 * r + l, 16 * slot : 16 * slot + 16] for l in range(3)]
            rows.append(jnp.concatenate(tiles, axis=1))
        return jnp.concatenate(rows, axis=0).astype(F32)

    depth = wh_ref.shape[0] // 2
    parts = [(c, x) for c in range(NC) for x in range(NX)]
    loads[0].wait()
    for slot in range(2):
        for c, x in parts:
            row = slot * depth + (c * NX + x) * 48
            wh_ref[row : row + 48, :] = block(hid_ref, c, x, slot)
    for load, source, target in ((loads[1], out_ref, wo_ref), (loads[2], que_ref, wq_ref)):
        load.wait()
        for c, x in parts:
            target[x * 48 : x * 48 + 48, c * 384 : c * 384 + 384] = block(source, c, x)
    vectors = [que_ref[c, x, 9].astype(F32) for c, x in parts]
    lines = [vector[0:1] for vector in vectors] + [vectors[0][1:2]]
    for i in range(3):
        logit_ref[128 * i : 128 * (i + 1)] = lines[i].reshape(128)
    for i in range(6):
        gain_ref[128 * i : 128 * (i + 1)] = lines[3 + i].reshape(128)
    loads[3].wait()
    columns = keys_ref.shape[1]
    keys_ref[...] = kv_ref[:, :columns]
    values_ref[...] = kv_ref[:, columns:]


def solution(mesh):
    nz = mesh.shape["pts"] // (NX * NC)
    ny = mesh.shape["head"]
    half_z = nz // 2

    def on_device(pool, index, labels, w_query, keys, values, w_out, out_gain, w_hidden, w_logit):
        points, columns = index.shape[0], keys.shape[1]
        width, hidden = w_hidden.shape
        latents = keys.shape[0] * nz * NX * NC
        heads = columns // HD
        vmem = pltpu.VMEM
        wide = (16, 2 * columns)
        forms = ((9, (32, 128)), (9, (16, 128)), (10, (16, 128)))
        shapes = [
            jax.ShapeDtypeStruct((NC, NX, count) + tile, BF16) for count, tile in forms
        ] + [jax.ShapeDtypeStruct((8, 2 * columns), F32)]
        buffers = []
        for count, tile in forms:
            buffers += [
                vmem((NC, NX, count) + tile, BF16),
                vmem((NX, count) + tile, BF16),
                vmem((NX, count) + tile, BF16),
                vmem((NX - 1, count) + tile, BF16),
                vmem((count,) + tile, BF16),
                vmem((nz - 1,) + tile, BF16),
            ]
        scratch = [vmem(shape.shape, shape.dtype) for shape in shapes] + [
            vmem((columns, pool.shape[0]), BF16),
            vmem((points,), jnp.int32),
            vmem((points,), jnp.int32),
            vmem((width,), BF16),
            vmem((hidden,), BF16),
            vmem((columns, width), BF16),
            vmem(keys.shape, BF16),
            vmem(keys.shape, BF16),
            vmem((ny, points, 128), BF16),
            vmem((ny, points // 2, 128), BF16),
            vmem((points, width), BF16),
            vmem((ny, columns, width), BF16),
            vmem((ny, width, hidden), BF16),
            vmem((ny, 1, hidden), F32),
            vmem((8, 2 * columns), F32),
            vmem((8, 2 * columns), F32),
            vmem((2, NX, half_z) + wide, BF16),
            vmem((points, columns), BF16),
            vmem((heads, latents, points), BF16),
            vmem((columns, points), BF16),
            vmem((ny, heads, points // 2, 128), BF16),
            vmem((2 * columns, latents), BF16),
            vmem((heads, latents, points), BF16),
            vmem((points, width), F32),
            vmem((points, width), BF16),
            vmem((ny, points, hidden), BF16),
            vmem((ny, points, hidden), F32),
            vmem((ny, points, hidden), BF16),
            *buffers,
            vmem((2, NX, half_z) + wide, BF16),
            vmem((NX, half_z) + wide, BF16),
            vmem((NX, half_z) + wide, BF16),
            vmem((NX - 1, half_z) + wide, BF16),
            vmem((half_z,) + wide, BF16),
            vmem((nz - 1,) + wide, BF16),
            vmem((2, 8, 2 * columns), F32),
            pltpu.SemaphoreType.DMA((16,)),
            pltpu.SemaphoreType.DMA((SEMAPHORES,)),
        ]
        whole = pl.BlockSpec(memory_space=pltpu.VMEM)
        sums = pl.pallas_call(
            lambda *refs: kernel(nz, ny, *refs),
            out_shape=shapes,
            in_specs=[pl.BlockSpec(memory_space=pl.ANY)] * 10,
            out_specs=[pl.BlockSpec(memory_space=pl.ANY)] * 4,
            scratch_shapes=scratch,
            compiler_params=pltpu.CompilerParams(
                collective_id=0, has_side_effects=True, vmem_limit_bytes=56 * 1024 * 1024
            ),
        )(pool.T, index, labels, out_gain, w_logit, w_query.T, keys, values, w_out, w_hidden)
        outs = pl.pallas_call(
            write_kernel,
            out_shape=[
                jax.ShapeDtypeStruct((columns, width), F32),
                jax.ShapeDtypeStruct((columns, width), F32),
                jax.ShapeDtypeStruct((width, hidden), F32),
                jax.ShapeDtypeStruct((hidden,), F32),
                jax.ShapeDtypeStruct((width,), F32),
                jax.ShapeDtypeStruct(keys.shape, F32),
                jax.ShapeDtypeStruct(keys.shape, F32),
            ],
            in_specs=[pl.BlockSpec(memory_space=pltpu.HBM)] * 4,
            out_specs=[whole] * 7,
            scratch_shapes=[vmem(shape.shape, shape.dtype) for shape in shapes]
            + [pltpu.SemaphoreType.DMA((4,))],
            compiler_params=pltpu.CompilerParams(vmem_limit_bytes=60 * 1024 * 1024),
        )(*sums)
        return (outs[0].T,) + tuple(outs[1:])

    return jax.shard_map(
        on_device,
        mesh=mesh,
        in_specs=(
            P("pts", "head"),
            P("pts"),
            P("pts"),
            P(None, "head"),
            P("pts", "head"),
            P("pts", "head"),
            P("head", None),
            P(),
            P(None, "head"),
            P("head"),
        ),
        out_specs=(
            P(None, "head"),
            P("head", None),
            P(None, "head"),
            P("head"),
            P(),
            P("pts", "head"),
            P("pts", "head"),
        ),
        check_vma=False,
    )
```
